128 devices in a mesh: dp: 4 (over x), expert: 32 (over y, z, core).
Axes of the slice: x: 4, y: 4, z: 4, core: 2. Of those that a mesh axis runs over, the one named last changes fastest.
Arguments:
- tokens: bfloat16 [16384, 2048], P(('dp', 'expert')), may hold values from -6 to 6
- cotangent: bfloat16 [16384, 2048], P(('dp', 'expert')), may hold values from -6 to 6
- expert_ids: int32 [16384, 8], P(('dp', 'expert')), may hold values from 0 to 63, all different within a row; in each aligned block of 128 rows (0 to 127, 128 to 255, ...) at most 24 rows name the same one
- gate_weights: bfloat16 [16384, 8], P(('dp', 'expert')), may hold values from 0.019897461 to 0.25
- token_counts: int32 [128], P(('dp', 'expert')), may hold values from 64 to 128, as said below
- gate_proj: bfloat16 [64, 2048, 768], P('expert'), may hold values from -0.125 to 0.125
- up_proj: bfloat16 [64, 2048, 768], P('expert'), may hold values from -0.125 to 0.125
- down_proj: bfloat16 [64, 768, 2048], P('expert'), may hold values from -0.21875 to 0.21875
Outputs:
- combined: bfloat16 [16384, 2048], P(('dp', 'expert'))
- tokens_grad: bfloat16 [16384, 2048], P(('dp', 'expert'))
- gates_grad: bfloat16 [16384, 8], P(('dp', 'expert'))
- gate_proj_grad: bfloat16 [64, 2048, 768], P('expert', 'dp')
- up_proj_grad: bfloat16 [64, 2048, 768], P('expert', 'dp')
- down_proj_grad: bfloat16 [64, 768, 2048], P('expert', None, 'dp')
The draws below stay inside these ranges and needn't reach their ends.
Inputs may be any that keep to these rules, and one draw needn't show every extreme that they name: `expert_ids`: each token names 8 different experts. Within the 128 rows of one device no expert is named by more than 24 rows, a bound that some block reaches. `token_counts`: rows of a device at positions below its count are live, the rest are padding. Some device is full and some holds exactly 64 live rows.
All inputs are finite; a program needn't handle non-finite values.
Results may differ from the reference program's by a relative error of at most 0.013.
Values may be sent and summed in bfloat16 or wider, within the bound.
No kernel may reach another device: no remote copies, remote signals or barrier semaphores. Data moves between devices by JAX's collectives and lax.ppermute only.
A program may use at most 192 MiB of HBM per device.

```python
import math
import jax
import jax.numpy as jnp
import numpy as np
from jax import lax

D = 2048
FF = 768
TOP = 8
TOK_DEV = 128
EXPERTS = 64
CAP = 24
TOKENS = 16384
N_DP = 4
N_EXPERT = 32


def draw_token_counts(key, part):
    key = jax.random.fold_in(key, 7)
    devices_all = N_DP * N_EXPERT
    first_key, second_key, third_key = jax.random.split(key, 3)
    values = jax.random.randint(first_key, (devices_all,), TOK_DEV // 2, TOK_DEV + 1)
    fullest = jax.random.randint(second_key, (), 0, devices_all)
    emptiest = (fullest + 1 + jax.random.randint(third_key, (), 0, devices_all - 1)) % devices_all
    positions = jnp.arange(devices_all)
    values = jnp.where(positions == fullest, TOK_DEV, values)
    values = jnp.where(positions == emptiest, TOK_DEV // 2, values)
    return values.astype(jnp.int32)


def levels(stream_key, shape, shards, least, top_value):
    loudness, own = 1.0, jax.random.fold_in(stream_key, 6)
    for axis_at, shards_of in shards:
        draws = jnp.exp(jax.random.uniform(jax.random.fold_in(own, axis_at), (shards_of,), jnp.float32, least / len(shards), top_value / len(shards)))
        loudness = loudness * jnp.repeat(draws, shape[axis_at] // shards_of).reshape([-1 if axis == axis_at else 1 for axis in range(len(shape))])
    return loudness


def assign_block(key, own, number, rows, number_of, top, reach, skew):
    ranking = jax.random.permutation(key, number_of)
    crowded, usual = shares(number_of, rows * top, reach, skew, True), shares(number_of, rows * top, reach, skew, False)
    places = jnp.arange(number_of)

    def named(sizes, offset_by):
        used = int((sizes > 0).sum())
        fixed = max(1, used // 4)
        shifted = fixed + (places - fixed + offset_by * (used - fixed)) % max(1, number_of - fixed)
        return jnp.zeros((number_of,), jnp.int32).at[ranking[jnp.where(places < fixed, places, shifted)]].set(jnp.asarray(sizes, jnp.int32))

    sizes = jnp.where(number % 4 == 0, named(crowded, number // 4), named(usual, number - number // 4 - 1))
    mixed = jax.random.permutation(jax.random.fold_in(own, 3), number_of)
    donor, receiver = mixed[0:number_of // 2 * 2:2], mixed[1:number_of // 2 * 2:2]
    margin = jnp.minimum(sizes[donor] - 1, reach - sizes[receiver]) // 2
    margin = jnp.where((donor == ranking[0]) | (receiver == ranking[0]) | (sizes[receiver] == 0), 0, jnp.maximum(margin, 0))
    shifted = jax.random.randint(jax.random.fold_in(own, 4), (number_of // 2,), 0, 1 << 20) % (margin + 1)
    sizes = sizes.at[donor].add(-shifted).at[receiver].add(shifted)
    items = jnp.searchsorted(jnp.cumsum(sizes), jnp.arange(rows * top), side="right").astype(jnp.int32)
    grid = items.reshape(top, rows).T
    grid = grid[jax.random.permutation(jax.random.fold_in(own, 1), rows)]
    offset_by = jax.random.randint(jax.random.fold_in(own, 2), (rows, 1), 0, top)
    return jnp.take_along_axis(grid, (jnp.arange(top)[None, :] + offset_by) % top, axis=1)


def shares(count, total, most, slope, full):
    loads = [(1 << 20) // math.isqrt(standing ** slope) + 1 for standing in range(1, count + 1)]
    largest = most if full else min(most, max(-(-total // count), total * loads[0] // sum(loads)))
    least = 1 if total - largest >= count - 1 else 0
    holding, surplus = [largest] + [least] * (count - 1), total - largest - least * (count - 1)
    while surplus > 0:
        free = [i for i in range(1, count) if holding[i] < largest] or [i for i in range(1, count) if holding[i] < most]
        pool, remaining = sum([loads[i] for i in free]), surplus
        for i in free:
            more = min(most - holding[i], max(1, remaining * loads[i] // pool), surplus)
            holding[i] = holding[i] + more
            surplus = surplus - more
    return np.array(holding)


def bell_draw(key, shape, width, bound, cuts=(), kind=jnp.bfloat16):
    array = jax.random.normal(key, shape, jnp.float32) * width
    if len(cuts) > 0:
        array = levels(key, shape, cuts, -0.22, 0.18) * array
    return jnp.clip(array, min=-bound, max=bound).astype(kind)


def setup_inputs(seed: int = 0) -> dict:
    key_list = jax.random.split(jax.random.key(seed), 9)
    tokens = bell_draw(key_list[0], (TOKENS, D), 1.0, 6.0, ((0, 128),))
    cotangent = bell_draw(key_list[1], (TOKENS, D), 1.0, 6.0, ((0, 128),))
    expert_ids_keys = jax.random.split(jax.random.fold_in(key_list[2], 1), TOKENS // TOK_DEV)
    expert_ids_turns = jax.random.permutation(jax.random.fold_in(key_list[2], 3), TOKENS // TOK_DEV)
    expert_ids = jax.vmap(lambda own, number: assign_block(jax.random.fold_in(key_list[2], 2), own, number, TOK_DEV, EXPERTS, TOP, CAP, 2))(expert_ids_keys, expert_ids_turns).reshape((TOKENS, TOP))
    gate_weights = jnp.clip(0.019897461 + 0.23010254 * jax.random.uniform(key_list[3], (TOKENS, TOP), jnp.float32) ** levels(key_list[3], (TOKENS, TOP), ((0, 128),), -0.2, 0.2), 0.019897461, 0.25).astype(jnp.bfloat16)
    token_counts = draw_token_counts(jax.random.fold_in(key_list[8], 71), 0)
    gate_proj = bell_draw(key_list[5], (EXPERTS, D, FF), D ** -0.5, 0.125, ((0, 32),))
    up_proj = bell_draw(key_list[6], (EXPERTS, D, FF), D ** -0.5, 0.125, ((0, 32),))
    down_proj = bell_draw(key_list[7], (EXPERTS, FF, D), FF ** -0.5, 0.21875, ((0, 32),))
    return dict(tokens=tokens, cotangent=cotangent, expert_ids=expert_ids, gate_weights=gate_weights, token_counts=token_counts, gate_proj=gate_proj, up_proj=up_proj, down_proj=down_proj)


def silu_parts(pre_gate):
    sigmoid_val = jax.nn.sigmoid(pre_gate)
    return pre_gate * sigmoid_val, sigmoid_val * (1.0 + pre_gate * (1.0 - sigmoid_val))


def forward_rows(row_block, gate_mat, up_mat, down_mat):
    pre_gate = jnp.dot(row_block, gate_mat, preferred_element_type=jnp.float32)
    pre_up = jnp.dot(row_block, up_mat, preferred_element_type=jnp.float32)
    activation, derivative = silu_parts(pre_gate)
    hidden = (activation * pre_up).astype(jnp.bfloat16)
    output = jnp.dot(hidden, down_mat, preferred_element_type=jnp.float32).astype(jnp.bfloat16)
    return pre_gate, pre_up, hidden, output


def backward_rows(row_block, pre_gate, pre_up, hidden, scaled, gate_mat, up_mat, down_mat):
    contract_last = (((1,), (1,)), ((), ()))
    contract_first = (((0,), (0,)), ((), ()))
    grad_hidden = lax.dot_general(scaled, down_mat, contract_last, preferred_element_type=jnp.float32)
    activation, derivative = silu_parts(pre_gate)
    grad_pregate = (grad_hidden * pre_up * derivative).astype(jnp.bfloat16)
    grad_preup = (grad_hidden * activation).astype(jnp.bfloat16)
    input_part = lax.dot_general(grad_pregate, gate_mat, contract_last, preferred_element_type=jnp.float32)
    input_part = input_part + lax.dot_general(grad_preup, up_mat, contract_last, preferred_element_type=jnp.float32)
    grad_gate = lax.dot_general(row_block, grad_pregate, contract_first, preferred_element_type=jnp.float32)
    grad_up = lax.dot_general(row_block, grad_preup, contract_first, preferred_element_type=jnp.float32)
    grad_down = lax.dot_general(hidden, scaled, contract_first, preferred_element_type=jnp.float32)
    return input_part.astype(jnp.bfloat16), grad_gate, grad_up, grad_down


def with_blank(values):
    return jnp.concatenate([values, jnp.zeros((1,) + values.shape[1:], values.dtype)], axis=0)


def reference(tokens, cotangent, expert_ids, gate_weights, token_counts, gate_proj, up_proj, down_proj):
    pairs_replica = N_EXPERT * TOK_DEV * TOP
    max_rows = N_EXPERT * CAP
    row_ids = jnp.arange(TOKENS, dtype=jnp.int32)
    is_live = (row_ids % TOK_DEV) < token_counts[row_ids // TOK_DEV]
    pair_live = jnp.repeat(is_live, TOP)
    sort_keys = jnp.where(pair_live, expert_ids.reshape(-1), EXPERTS).astype(jnp.int32)
    sort_keys = sort_keys.reshape(N_DP, pairs_replica)
    orders = []
    starts = []
    counts = []
    for replica in range(N_DP):
        ordering = jnp.argsort(sort_keys[replica], stable=True).astype(jnp.int32) + replica * pairs_replica
        expert_load = jax.ops.segment_sum(jnp.ones((pairs_replica,), jnp.int32), sort_keys[replica], num_segments=EXPERTS + 1)[:EXPERTS]
        orders.append(jnp.concatenate([ordering, jnp.full((max_rows,), TOKENS * TOP, jnp.int32)]))
        starts.append((jnp.cumsum(expert_load) - expert_load).astype(jnp.int32))
        counts.append(expert_load.astype(jnp.int32))
    order_table = jnp.stack(orders)
    start_table = jnp.stack(starts)
    count_table = jnp.stack(counts)
    tokens_pad = with_blank(tokens)
    cot_pad = with_blank(cotangent)
    gate_pad = with_blank(gate_weights.reshape(-1))

    def per_expert(carried, expert):
        combined_sum, input_sum, products = carried
        gate_mat = gate_proj[expert]
        up_mat = up_proj[expert]
        down_mat = down_proj[expert]
        partial_gate = jnp.zeros((D, FF), jnp.float32)
        partial_up = jnp.zeros((D, FF), jnp.float32)
        partial_down = jnp.zeros((FF, D), jnp.float32)
        for replica in range(N_DP):
            pair_rows = lax.dynamic_slice_in_dim(order_table[replica], start_table[replica, expert], max_rows)
            in_use = jnp.arange(max_rows, dtype=jnp.int32) < count_table[replica, expert]
            pair_rows = jnp.where(in_use, pair_rows, TOKENS * TOP).astype(jnp.int32)
            token_rows = (pair_rows // TOP).astype(jnp.int32)
            row_block = tokens_pad[token_rows]
            cot_block = cot_pad[token_rows]
            gate_block = gate_pad[pair_rows]
            pre_gate, pre_up, hidden, output = forward_rows(row_block, gate_mat, up_mat, down_mat)
            scaled = (gate_block.astype(jnp.float32)[:, None] * cot_block.astype(jnp.float32)).astype(jnp.bfloat16)
            product = jnp.sum(output.astype(jnp.float32) * cot_block.astype(jnp.float32), axis=1).astype(jnp.bfloat16)
            input_part, grad_gate, grad_up, grad_down = backward_rows(row_block, pre_gate, pre_up, hidden, scaled, gate_mat, up_mat, down_mat)
            combined_sum = combined_sum.at[token_rows].add(gate_block.astype(jnp.float32)[:, None] * output.astype(jnp.float32))
            input_sum = input_sum.at[token_rows].add(input_part.astype(jnp.float32))
            products = products.at[pair_rows].set(product)
            partial_gate = partial_gate + lax.optimization_barrier(grad_gate.astype(jnp.bfloat16)).astype(jnp.float32)
            partial_up = partial_up + lax.optimization_barrier(grad_up.astype(jnp.bfloat16)).astype(jnp.float32)
            partial_down = partial_down + lax.optimization_barrier(grad_down.astype(jnp.bfloat16)).astype(jnp.float32)
        outputs = (partial_gate.astype(jnp.bfloat16), partial_up.astype(jnp.bfloat16), partial_down.astype(jnp.bfloat16))
        return (combined_sum, input_sum, products), outputs

    start_carry = (jnp.zeros((TOKENS + 1, D), jnp.float32), jnp.zeros((TOKENS + 1, D), jnp.float32), jnp.zeros((TOKENS * TOP + 1,), jnp.bfloat16))
    finals, stacked = lax.scan(per_expert, start_carry, jnp.arange(EXPERTS, dtype=jnp.int32))
    combined_sum, input_sum, products = finals
    combined = combined_sum[:TOKENS].astype(jnp.bfloat16)
    tokens_grad = input_sum[:TOKENS].astype(jnp.bfloat16)
    gates_grad = products[:TOKENS * TOP].reshape(TOKENS, TOP)
    return combined, tokens_grad, gates_grad, stacked[0], stacked[1], stacked[2]
```

```python
import jax
import jax.numpy as jnp
from jax import lax
from jax.sharding import PartitionSpec as P

F32 = jnp.float32
BF16 = jnp.bfloat16
CONTRACT_FIRST = (((0,), (0,)), ((), ()))
CONTRACT_LAST = (((1,), (1,)), ((), ()))


def dot(a, b, dims=(((1,), (0,)), ((), ()))):
    return lax.dot_general(a, b, dims, preferred_element_type=F32)


def silu_parts(pre_gate):
    s = jax.nn.sigmoid(pre_gate)
    return pre_gate * s, s * (1.0 + pre_gate * (1.0 - s))


def slot_masks(expert_ids, gate_weights, live_count, experts_total, capacity):
    tok_dev = expert_ids.shape[0]
    live = lax.broadcasted_iota(jnp.int32, (experts_total, tok_dev), 1) < live_count
    labels = lax.broadcasted_iota(jnp.int32, (experts_total, 1, tok_dev), 0)
    hits = expert_ids.T[None] == labels
    names = jnp.any(hits, axis=1) & live
    gates = jnp.sum(jnp.where(hits, gate_weights.T[None].astype(F32), 0.0), axis=1)
    before = (
        lax.broadcasted_iota(jnp.int32, (tok_dev, tok_dev), 0)
        < lax.broadcasted_iota(jnp.int32, (tok_dev, tok_dev), 1)
    )
    rank = dot(names.astype(BF16), before.astype(BF16)).astype(jnp.int32)
    column = lax.broadcasted_iota(jnp.int32, (1, capacity, 1), 1)
    mask = names[:, None, :] & (rank[:, None, :] == column)
    return mask, gates


def exchange(rows, group):
    rows = rows.reshape(group, -1, rows.shape[-1])
    got = lax.all_to_all(rows, "expert", split_axis=0, concat_axis=0, tiled=True)
    return got.reshape(-1, rows.shape[-1])


def local(tokens, cotangent, expert_ids, gate_weights, token_counts, gate_proj, up_proj, down_proj):
    group = lax.axis_size("expert")
    local_experts, model_dim, hidden_dim = gate_proj.shape
    tok_dev, per_token = expert_ids.shape
    experts_total = group * local_experts
    capacity = 3 * tok_dev * per_token // (2 * experts_total)
    rows = group * capacity

    mask, gates = slot_masks(expert_ids, gate_weights, token_counts[0], experts_total, capacity)
    by_expert = mask.reshape(group, local_experts, capacity, tok_dev)
    gates_by = gates.reshape(group, local_experts, 1, tok_dev)
    places, weights = [], []
    for e in range(local_experts):
        here = by_expert[:, e]
        places.append(here.astype(BF16).reshape(rows, tok_dev))
        weights.append(jnp.where(here, gates_by[:, e], 0.0).astype(BF16).reshape(rows, tok_dev))

    got_tokens, got_scaled = [], []
    for e in range(local_experts):
        got_tokens.append(exchange(dot(places[e], tokens).astype(BF16), group))
        got_scaled.append(exchange(dot(weights[e], cotangent).astype(BF16), group))

    combined = jnp.zeros((tok_dev, model_dim), F32)
    tokens_grad = jnp.zeros((tok_dev, model_dim), F32)
    products = []
    reduced = []
    for e in range(local_experts):
        x, scaled = got_tokens[e], got_scaled[e]
        gate_mat, up_mat, down_mat = gate_proj[e], up_proj[e], down_proj[e]
        pre_gate = dot(x, gate_mat)
        pre_up = dot(x, up_mat)
        activation, derivative = silu_parts(pre_gate)
        hidden = (activation * pre_up).astype(BF16)
        out = exchange(dot(hidden, down_mat).astype(BF16), group)
        grad_hidden = dot(scaled, down_mat, CONTRACT_LAST)
        grad_pregate = (grad_hidden * pre_up * derivative).astype(BF16)
        grad_preup = (grad_hidden * activation).astype(BF16)
        grads = jnp.concatenate(
            [
                dot(scaled, hidden, CONTRACT_FIRST).astype(BF16),
                dot(x, grad_pregate, CONTRACT_FIRST).astype(BF16),
                dot(x, grad_preup, CONTRACT_FIRST).astype(BF16),
            ],
            axis=1,
        )
        reduced.append(lax.psum_scatter(grads, "dp", scatter_dimension=0, tiled=True))
        part = exchange(
            (dot(grad_pregate, gate_mat, CONTRACT_LAST) + dot(grad_preup, up_mat, CONTRACT_LAST)).astype(BF16),
            group,
        )
        combined = combined + dot(weights[e], out, CONTRACT_FIRST)
        tokens_grad = tokens_grad + dot(places[e], part, CONTRACT_FIRST)
        product = dot(out, cotangent, CONTRACT_LAST).reshape(group, capacity, tok_dev)
        products.append(jnp.sum(jnp.where(by_expert[:, e], product, 0.0), axis=1))

    per_expert = jnp.stack(products, axis=1).reshape(experts_total, 1, tok_dev)
    labels = lax.broadcasted_iota(jnp.int32, (experts_total, 1, tok_dev), 0)
    gates_grad = jnp.sum(jnp.where(expert_ids.T[None] == labels, per_expert, 0.0), axis=0).T
    reduced = jnp.stack(reduced)
    return (
        combined.astype(BF16),
        tokens_grad.astype(BF16),
        gates_grad.astype(BF16),
        reduced[:, :, hidden_dim : 2 * hidden_dim],
        reduced[:, :, 2 * hidden_dim :],
        jnp.swapaxes(reduced[:, :, :hidden_dim], 1, 2),
    )


def solution(mesh):
    both = ("dp", "expert")
    return jax.shard_map(
        local,
        mesh=mesh,
        in_specs=(
            P(both, None),
            P(both, None),
            P(both, None),
            P(both, None),
            P(both),
            P("expert", None, None),
            P("expert", None, None),
            P("expert", None, None),
        ),
        out_specs=(
            P(both, None),
            P(both, None),
            P(both, None),
            P("expert", "dp", None),
            P("expert", "dp", None),
            P("expert", None, "dp"),
        ),
        check_vma=False,
    )
```

```python
import functools

import jax
import jax.numpy as jnp
from jax import lax
from jax.experimental import pallas as pl
from jax.experimental.pallas import tpu as pltpu
from jax.sharding import PartitionSpec as P

F32 = jnp.float32
BF16 = jnp.bfloat16
CONTRACT_FIRST = (((0,), (0,)), ((), ()))
CONTRACT_LAST = (((1,), (1,)), ((), ()))
NOBODY = 255.0
META_ROWS = 16


def dot(a, b, dims=(((1,), (0,)), ((), ()))):
    return lax.dot_general(a, b, dims, preferred_element_type=F32)


def dispatch_kernel(top, capacity, first_ref, block_ref, *out_refs):
    sources, _, model_dim = block_ref.shape
    tok_dev = 128
    experts = len(out_refs) // 2
    before = (
        lax.broadcasted_iota(jnp.int32, (tok_dev, tok_dev), 0)
        < lax.broadcasted_iota(jnp.int32, (tok_dev, tok_dev), 1)
    ).astype(BF16)
    column = lax.broadcasted_iota(jnp.int32, (capacity, tok_dev), 0).astype(F32)
    picked = []
    for j in range(sources):
        meta = block_ref[j, 2 * tok_dev :, :].astype(F32)[0:1]
        places, weights = [], []
        for e in range(experts):
            expert = (first_ref[0] + e).astype(F32)
            name = jnp.zeros((1, tok_dev), F32)
            gate = jnp.zeros((1, tok_dev), F32)
            for k in range(top):
                hit = meta[:, k * tok_dev : (k + 1) * tok_dev] == expert
                name = jnp.where(hit, 1.0, name)
                gate = jnp.where(hit, meta[:, (top + k) * tok_dev : (top + k + 1) * tok_dev], gate)
            rank = dot(jnp.broadcast_to(name, (16, tok_dev)).astype(BF16), before)[0:1]
            here = (rank == column) & (name > 0.0)
            places.append(jnp.where(here, 1.0, 0.0))
            weights.append(jnp.where(here, gate, 0.0))
        rows = dot(jnp.concatenate(places).astype(BF16), block_ref[j, :tok_dev, :])
        scaled = dot(jnp.concatenate(weights).astype(BF16), block_ref[j, tok_dev : 2 * tok_dev, :])
        picked.append((rows, scaled))
    for e in range(experts):
        span = slice(e * capacity, (e + 1) * capacity)
        for which in range(2):
            out_refs[2 * e + which][...] = jnp.concatenate([pair[which][span] for pair in picked]).astype(BF16)


def dispatch(gathered, first_expert, experts, top, capacity):
    group, height, model_dim = gathered.shape
    step = 2
    rows = jax.ShapeDtypeStruct((group * capacity, model_dim), BF16)
    out = pl.BlockSpec((step * capacity, model_dim), lambda s: (s, 0))
    return pl.pallas_call(
        functools.partial(dispatch_kernel, top, capacity),
        grid=(group // step,),
        in_specs=[
            pl.BlockSpec(memory_space=pltpu.SMEM),
            pl.BlockSpec((step, height, model_dim), lambda s: (s, 0, 0)),
        ],
        out_specs=[out] * (2 * experts),
        out_shape=[rows] * (2 * experts),
        compiler_params=pltpu.CompilerParams(vmem_limit_bytes=48 << 20),
        cost_estimate=pl.CostEstimate(
            flops=4 * experts * group * capacity * 128 * model_dim,
            bytes_accessed=gathered.size * 2 + 4 * experts * group * capacity * model_dim,
            transcendentals=0,
        ),
    )(first_expert, gathered)


def expert_kernel(x_ref, scaled_ref, gate_ref, up_ref, down_ref, back_ref, grads_ref, xt, st, acc_out, acc_part):
    tile = pl.program_id(0)
    group = back_ref.shape[0]
    capacity = back_ref.shape[1] // 2
    shards, _, shard_rows, _ = grads_ref.shape

    @pl.when(tile == 0)
    def _():
        xt[...] = x_ref[...].T
        st[...] = scaled_ref[...].T

    pre_gate = dot(x_ref[...], gate_ref[...])
    pre_up = dot(x_ref[...], up_ref[...])
    grad_hidden = dot(scaled_ref[...], down_ref[...], CONTRACT_LAST)
    s = jax.nn.sigmoid(pre_gate)
    activation = pre_gate * s
    hidden = (activation * pre_up).astype(BF16)
    grad_pregate = (grad_hidden * pre_up * (s * (1.0 + pre_gate * (1.0 - s)))).astype(BF16)
    grad_preup = (grad_hidden * activation).astype(BF16)

    for which, (left, right) in enumerate(((xt, grad_pregate), (xt, grad_preup), (st, hidden))):
        for r in range(shards):
            rows = slice(r * shard_rows, (r + 1) * shard_rows)
            grads_ref[r, which] = dot(left[rows, :], right).astype(BF16)

    out = dot(hidden, down_ref[...])
    part = dot(grad_pregate, gate_ref[...], CONTRACT_LAST) + dot(grad_preup, up_ref[...], CONTRACT_LAST)

    @pl.when(tile == 0)
    def _():
        acc_out[...] = out
        acc_part[...] = part

    @pl.when(tile > 0)
    def _():
        acc_out[...] += out
        acc_part[...] += part

    @pl.when(tile == pl.num_programs(0) - 1)
    def _():
        for source in range(group):
            rows = slice(source * capacity, (source + 1) * capacity)
            back_ref[source] = jnp.concatenate([acc_out[rows, :], acc_part[rows, :]]).astype(BF16)


def run_expert(x, scaled, gate_proj, up_proj, down_proj, e, group, shards):
    rows, model_dim = x.shape
    hidden_dim = gate_proj.shape[2]
    capacity = rows // group
    tile = 256
    whole = pl.BlockSpec((rows, model_dim), lambda f: (0, 0), pipeline_mode=pl.Buffered(1))
    return pl.pallas_call(
        expert_kernel,
        grid=(hidden_dim // tile,),
        in_specs=[
            whole,
            whole,
            pl.BlockSpec((None, model_dim, tile), lambda f: (e, 0, f)),
            pl.BlockSpec((None, model_dim, tile), lambda f: (e, 0, f)),
            pl.BlockSpec((None, tile, model_dim), lambda f: (e, f, 0)),
        ],
        out_specs=[
            pl.BlockSpec((group, 2 * capacity, model_dim), lambda f: (0, 0, 0), pipeline_mode=pl.Buffered(1)),
            pl.BlockSpec((shards, 3, model_dim // shards, tile), lambda f: (0, 0, 0, f)),
        ],
        out_shape=[
            jax.ShapeDtypeStruct((group, 2 * capacity, model_dim), BF16),
            jax.ShapeDtypeStruct((shards, 3, model_dim // shards, hidden_dim), BF16),
        ],
        scratch_shapes=[
            pltpu.VMEM((model_dim, rows), BF16),
            pltpu.VMEM((model_dim, rows), BF16),
            pltpu.VMEM((rows, model_dim), F32),
            pltpu.VMEM((rows, model_dim), F32),
        ],
        compiler_params=pltpu.CompilerParams(vmem_limit_bytes=60 << 20),
        cost_estimate=pl.CostEstimate(
            flops=18 * rows * model_dim * hidden_dim,
            bytes_accessed=8 * rows * model_dim + 12 * model_dim * hidden_dim,
            transcendentals=rows * hidden_dim,
        ),
    )(x, scaled, gate_proj, up_proj, down_proj)


def local(tokens, cotangent, expert_ids, gate_weights, token_counts, gate_proj, up_proj, down_proj):
    group = lax.axis_size("expert")
    shards = lax.axis_size("dp")
    local_experts, model_dim, hidden_dim = gate_proj.shape
    tok_dev, top = expert_ids.shape
    experts_total = group * local_experts
    capacity = 3 * tok_dev * top // (2 * experts_total)

    live = lax.broadcasted_iota(jnp.int32, (tok_dev, top), 0) < token_counts[0]
    named = jnp.where(live, expert_ids, int(NOBODY))
    meta = jnp.concatenate([named.T.astype(BF16).reshape(1, -1), gate_weights.T.reshape(1, -1)], axis=1)
    meta = jnp.broadcast_to(meta, (META_ROWS, model_dim))
    mine = jnp.concatenate([tokens, cotangent, meta])
    gathered = lax.all_gather(mine[None], "expert", axis=0, tiled=True)

    labels = lax.broadcasted_iota(jnp.int32, (1, 1, experts_total), 2)
    hits = named[:, :, None] == labels
    names = jnp.any(hits, axis=1)
    gates = jnp.sum(jnp.where(hits, gate_weights.astype(F32)[:, :, None], 0.0), axis=1)
    after = (
        lax.broadcasted_iota(jnp.int32, (tok_dev, tok_dev), 0)
        > lax.broadcasted_iota(jnp.int32, (tok_dev, tok_dev), 1)
    )
    rank = dot(after.astype(BF16), names.astype(BF16)).astype(jnp.int32)
    column = lax.broadcasted_iota(jnp.int32, (1, 1, 2 * capacity), 2)

    first = (lax.axis_index("expert") * local_experts).astype(jnp.int32).reshape(1)
    picked = dispatch(gathered, first, local_experts, top, capacity)

    sums = jnp.zeros((2 * tok_dev, model_dim), F32)
    products = []
    reduced = []
    for e in range(local_experts):
        back, grads = run_expert(
            picked[2 * e], picked[2 * e + 1], gate_proj, up_proj, down_proj, e, group, shards
        )
        reduced.append(lax.psum_scatter(grads, "dp", scatter_dimension=0, tiled=False))
        got = lax.all_to_all(back, "expert", split_axis=0, concat_axis=0, tiled=True)
        got = got.reshape(-1, model_dim)
        names_e, rank_e, gates_e = (
            v.reshape(tok_dev, group, local_experts)[:, :, e, None] for v in (names, rank, gates)
        )
        here_out = names_e & (rank_e == column)
        here_part = names_e & (rank_e + capacity == column)
        picks = jnp.concatenate(
            [
                jnp.where(here_out, gates_e, 0.0).astype(BF16).reshape(tok_dev, -1),
                here_part.astype(BF16).reshape(tok_dev, -1),
            ]
        )
        sums = sums + dot(picks, got)
        product = dot(cotangent, got, CONTRACT_LAST).reshape(tok_dev, group, 2 * capacity)
        products.append(jnp.sum(jnp.where(here_out, product, 0.0), axis=2))

    per_expert = jnp.stack(products, axis=2).reshape(tok_dev, 1, experts_total)
    gates_grad = jnp.sum(jnp.where(hits, per_expert, 0.0), axis=2)
    reduced = jnp.stack(reduced)
    return (
        sums[:tok_dev].astype(BF16),
        sums[tok_dev:].astype(BF16),
        gates_grad.astype(BF16),
        reduced[:, 0],
        reduced[:, 1],
        jnp.swapaxes(reduced[:, 2], 1, 2),
    )


def solution(mesh):
    both = ("dp", "expert")
    return jax.shard_map(
        local,
        mesh=mesh,
        in_specs=(
            P(both, None),
            P(both, None),
            P(both, None),
            P(both, None),
            P(both),
            P("expert", None, None),
            P("expert", None, None),
            P("expert", None, None),
        ),
        out_specs=(
            P(both, None),
            P(both, None),
            P(both, None),
            P("expert", "dp", None),
            P("expert", "dp", None),
            P("expert", None, "dp"),
        ),
        check_vma=False,
    )
```

```python
import functools

import jax
import jax.numpy as jnp
from jax import lax
from jax.experimental import pallas as pl
from jax.experimental.pallas import tpu as pltpu
from jax.sharding import PartitionSpec as P

F32 = jnp.float32
BF16 = jnp.bfloat16
CONTRACT_FIRST = (((0,), (0,)), ((), ()))
CONTRACT_LAST = (((1,), (1,)), ((), ()))
NOBODY = -1


def dot(a, b, dims=(((1,), (0,)), ((), ()))):
    return lax.dot_general(a, b, dims, preferred_element_type=F32)


def grads_kernel(rows_ref, gate_ref, up_ref, down_ref, grads_ref, hidden_ref, pregate_ref, preup_ref, x, xt, sc, st):
    shards, _, shard_rows, _ = grads_ref.shape
    group, height, _ = rows_ref.shape
    capacity = height // 2

    @pl.when(pl.program_id(0) == 0)
    def _():
        for pair in range(0, group, 2):
            blocks = [rows_ref[pair + j].astype(F32) for j in range(2)]
            span = slice(pair * capacity, (pair + 2) * capacity)
            sc[span, :] = jnp.concatenate([block[:capacity] for block in blocks]).astype(BF16)
            x[span, :] = jnp.concatenate([block[capacity:] for block in blocks]).astype(BF16)
        xt[...] = x[...].T
        st[...] = sc[...].T

    pre_gate = dot(x[...], gate_ref[...])
    pre_up = dot(x[...], up_ref[...])
    grad_hidden = dot(sc[...], down_ref[...], CONTRACT_LAST)
    s = jax.nn.sigmoid(pre_gate)
    activation = pre_gate * s
    hidden = (activation * pre_up).astype(BF16)
    grad_pregate = (grad_hidden * pre_up * (s * (1.0 + pre_gate * (1.0 - s)))).astype(BF16)
    grad_preup = (grad_hidden * activation).astype(BF16)
    hidden_ref[...] = hidden
    pregate_ref[...] = grad_pregate
    preup_ref[...] = grad_preup
    for which, (left, right) in enumerate(((xt, grad_pregate), (xt, grad_preup), (st, hidden))):
        for r in range(shards):
            rows = slice(r * shard_rows, (r + 1) * shard_rows)
            grads_ref[r, which] = dot(left[rows, :], right).astype(BF16)


def expert_grads(got, gate_proj, up_proj, down_proj, e, shards):
    group, height, model_dim = got.shape
    rows = group * height // 2
    hidden_dim = gate_proj.shape[2]
    tile = 256
    narrow = pl.BlockSpec((rows, tile), lambda f: (0, f))
    return pl.pallas_call(
        grads_kernel,
        grid=(hidden_dim // tile,),
        in_specs=[
            pl.BlockSpec(got.shape, lambda f: (0, 0, 0), pipeline_mode=pl.Buffered(1)),
            pl.BlockSpec((None, model_dim, tile), lambda f: (e, 0, f)),
            pl.BlockSpec((None, model_dim, tile), lambda f: (e, 0, f)),
            pl.BlockSpec((None, tile, model_dim), lambda f: (e, f, 0)),
        ],
        out_specs=[
            pl.BlockSpec((shards, 3, model_dim // shards, tile), lambda f: (0, 0, 0, f)),
            narrow,
            narrow,
            narrow,
        ],
        out_shape=[jax.ShapeDtypeStruct((shards, 3, model_dim // shards, hidden_dim), BF16)]
        + [jax.ShapeDtypeStruct((rows, hidden_dim), BF16)] * 3,
        scratch_shapes=[pltpu.VMEM((rows, model_dim), BF16), pltpu.VMEM((model_dim, rows), BF16)] * 2,
        compiler_params=pltpu.CompilerParams(vmem_limit_bytes=56 << 20),
        cost_estimate=pl.CostEstimate(
            flops=12 * rows * model_dim * hidden_dim,
            bytes_accessed=4 * rows * model_dim + 12 * model_dim * hidden_dim + 6 * rows * hidden_dim,
            transcendentals=rows * hidden_dim,
        ),
    )(got, gate_proj, up_proj, down_proj)


def returns_kernel(hidden_ref, pregate_ref, preup_ref, gate_ref, up_ref, down_ref, back_ref):
    group, height, _ = back_ref.shape
    capacity = height // 2
    out = dot(hidden_ref[...], down_ref[...])
    part = dot(pregate_ref[...], gate_ref[...], CONTRACT_LAST) + dot(preup_ref[...], up_ref[...], CONTRACT_LAST)
    for source in range(group):
        rows = slice(source * capacity, (source + 1) * capacity)
        back_ref[source] = jnp.concatenate([out[rows], part[rows]]).astype(BF16)


def expert_returns(hidden, pregate, preup, gate_proj, up_proj, down_proj, e, group):
    rows, hidden_dim = hidden.shape
    model_dim = gate_proj.shape[1]
    capacity = rows // group
    tile = 512
    whole = pl.BlockSpec((rows, hidden_dim), lambda d: (0, 0), pipeline_mode=pl.Buffered(1))
    return pl.pallas_call(
        returns_kernel,
        grid=(model_dim // tile,),
        in_specs=[
            whole,
            whole,
            whole,
            pl.BlockSpec((None, tile, hidden_dim), lambda d: (e, d, 0)),
            pl.BlockSpec((None, tile, hidden_dim), lambda d: (e, d, 0)),
            pl.BlockSpec((None, hidden_dim, tile), lambda d: (e, 0, d)),
        ],
        out_specs=pl.BlockSpec((group, 2 * capacity, tile), lambda d: (0, 0, d)),
        out_shape=jax.ShapeDtypeStruct((group, 2 * capacity, model_dim), BF16),
        compiler_params=pltpu.CompilerParams(vmem_limit_bytes=48 << 20),
        cost_estimate=pl.CostEstimate(
            flops=600 * rows * model_dim * hidden_dim,
            bytes_accessed=4 * rows * model_dim + 6 * model_dim * hidden_dim + 6 * rows * hidden_dim,
            transcendentals=0,
        ),
    )(hidden, pregate, preup, gate_proj, up_proj, down_proj)


def place_kernel(*refs):
    *reduced, gate_ref, up_ref, down_ref = refs
    for e, ref in enumerate(reduced):
        gate_ref[e] = ref[0]
        up_ref[e] = ref[1]
        down_ref[e] = ref[2].T


def place_grads(reduced):
    experts = len(reduced)
    _, shard_rows, hidden_dim = reduced[0].shape
    tile = 256
    straight = pl.BlockSpec((experts, shard_rows, tile), lambda f: (0, 0, f))
    return pl.pallas_call(
        place_kernel,
        grid=(hidden_dim // tile,),
        in_specs=[pl.BlockSpec((3, shard_rows, tile), lambda f: (0, 0, f))] * experts,
        out_specs=[straight, straight, pl.BlockSpec((experts, tile, shard_rows), lambda f: (0, f, 0))],
        out_shape=[
            jax.ShapeDtypeStruct((experts, shard_rows, hidden_dim), BF16),
            jax.ShapeDtypeStruct((experts, shard_rows, hidden_dim), BF16),
            jax.ShapeDtypeStruct((experts, hidden_dim, shard_rows), BF16),
        ],
        compiler_params=pltpu.CompilerParams(vmem_limit_bytes=32 << 20),
        cost_estimate=pl.CostEstimate(
            flops=0, bytes_accessed=12 * experts * shard_rows * hidden_dim, transcendentals=0
        ),
    )(*reduced)


def exchange(rows):
    return lax.all_to_all(rows, "expert", split_axis=0, concat_axis=0, tiled=True)


def local(tokens, cotangent, expert_ids, gate_weights, token_counts, gate_proj, up_proj, down_proj):
    group = lax.axis_size("expert")
    shards = lax.axis_size("dp")
    local_experts, model_dim, hidden_dim = gate_proj.shape
    tok_dev, top = expert_ids.shape
    experts_total = group * local_experts
    capacity = 3 * tok_dev * top // (2 * experts_total)

    live = lax.broadcasted_iota(jnp.int32, (tok_dev, top), 0) < token_counts[0]
    named = jnp.where(live, expert_ids, NOBODY)
    labels = lax.broadcasted_iota(jnp.int32, (experts_total, 1, 1), 0)
    hits = named.T[None] == labels
    names = jnp.any(hits, axis=1)
    gates = jnp.sum(jnp.where(hits, gate_weights.T[None].astype(F32), 0.0), axis=1)
    before = (
        lax.broadcasted_iota(jnp.int32, (tok_dev, tok_dev), 0)
        < lax.broadcasted_iota(jnp.int32, (tok_dev, tok_dev), 1)
    )
    rank = dot(names.astype(BF16), before.astype(BF16)).astype(jnp.int32)
    names, gates, rank = (v.reshape(group, local_experts, 1, tok_dev) for v in (names, gates, rank))
    column = lax.broadcasted_iota(jnp.int32, (1, 2 * capacity, 1), 1)
    stacked = jnp.concatenate([cotangent, tokens])

    masks, picks = [], []
    for e in range(local_experts):
        masks.append(names[:, e] & (rank[:, e] == column))
        second = names[:, e] & (rank[:, e] + capacity == column)
        picks.append(
            jnp.concatenate([jnp.where(masks[e], gates[:, e], 0.0).astype(BF16), second.astype(BF16)], axis=2)
            .reshape(-1, 2 * tok_dev)
        )
    sent = [dot(picks[e], stacked).astype(BF16).reshape(group, 2 * capacity, model_dim) for e in range(local_experts)]

    got = exchange(sent[0])
    returned, reduced = [], []
    back = None
    for e in range(local_experts):
        arriving = exchange(sent[e + 1] if e + 1 < local_experts else back)
        grads, hidden, pregate, preup = expert_grads(got, gate_proj, up_proj, down_proj, e, shards)
        reduced.append(lax.psum_scatter(grads, "dp", scatter_dimension=0, tiled=False))
        if e + 1 < local_experts:
            got = arriving
        else:
            returned.append(arriving)
        back = expert_returns(hidden, pregate, preup, gate_proj, up_proj, down_proj, e, group)
    returned.append(exchange(back))

    sums = jnp.zeros((2 * tok_dev, model_dim), F32)
    products = []
    for e, rows in enumerate(returned):
        rows = rows.reshape(-1, model_dim)
        sums = sums + dot(picks[e], rows, CONTRACT_FIRST)
        product = dot(rows, cotangent, CONTRACT_LAST).reshape(group, 2 * capacity, tok_dev)
        products.append(jnp.sum(jnp.where(masks[e], product, 0.0), axis=1))

    per_expert = jnp.stack(products, axis=1).reshape(experts_total, 1, tok_dev)
    gates_grad = jnp.sum(jnp.where(hits, per_expert, 0.0), axis=0).T
    return (
        sums[:tok_dev].astype(BF16),
        sums[tok_dev:].astype(BF16),
        gates_grad.astype(BF16),
        *place_grads(reduced),
    )


def solution(mesh):
    both = ("dp", "expert")
    return jax.shard_map(
        local,
        mesh=mesh,
        in_specs=(
            P(both, None),
            P(both, None),
            P(both, None),
            P(both, None),
            P(both),
            P("expert", None, None),
            P("expert", None, None),
            P("expert", None, None),
        ),
        out_specs=(
            P(both, None),
            P(both, None),
            P(both, None),
            P("expert", "dp", None),
            P("expert", "dp", None),
            P("expert", None, "dp"),
        ),
        check_vma=False,
    )
```

```python
import functools

import jax
import jax.numpy as jnp
from jax import lax
from jax.experimental import pallas as pl
from jax.experimental.pallas import tpu as pltpu
from jax.sharding import PartitionSpec as P

F32 = jnp.float32
BF16 = jnp.bfloat16
CONTRACT_FIRST = (((0,), (0,)), ((), ()))
CONTRACT_LAST = (((1,), (1,)), ((), ()))
NOBODY = -1


def dot(a, b, dims=(((1,), (0,)), ((), ()))):
    return lax.dot_general(a, b, dims, preferred_element_type=F32)


def dispatch_kernel(capacity, first_ref, block_ref, *out_refs):
    sources = block_ref.shape[0]
    tok_dev = 128
    experts = len(out_refs) // 2
    before = (
        lax.broadcasted_iota(jnp.int32, (tok_dev, tok_dev), 0)
        < lax.broadcasted_iota(jnp.int32, (tok_dev, tok_dev), 1)
    ).astype(BF16)
    column = lax.broadcasted_iota(jnp.int32, (capacity, tok_dev), 0).astype(F32)
    names, gates = [], []
    for j in range(sources):
        routing = block_ref[j, 2 * tok_dev :, :tok_dev].astype(F32)
        ids, given = routing[:8], routing[8:]
        for e in range(experts):
            hit = ids == (first_ref[0] + e).astype(F32)
            names.append(jnp.max(jnp.where(hit, 1.0, 0.0), axis=0, keepdims=True))
            gates.append(jnp.sum(jnp.where(hit, given, 0.0), axis=0, keepdims=True))
    names = jnp.concatenate(names)
    ranks = dot(names.astype(BF16), before)
    picked = []
    for j in range(sources):
        places, weights = [], []
        for e in range(experts):
            row = slice(j * experts + e, j * experts + e + 1)
            here = (ranks[row] == column) & (names[row] > 0.0)
            places.append(jnp.where(here, 1.0, 0.0))
            weights.append(jnp.where(here, gates[j * experts + e], 0.0))
        rows = dot(jnp.concatenate(places).astype(BF16), block_ref[j, :tok_dev, :])
        scaled = dot(jnp.concatenate(weights).astype(BF16), block_ref[j, tok_dev : 2 * tok_dev, :])
        picked.append((rows, scaled))
    for e in range(experts):
        span = slice(e * capacity, (e + 1) * capacity)
        for which in range(2):
            out_refs[2 * e + which][...] = jnp.concatenate([pair[which][span] for pair in picked]).astype(BF16)


def dispatch(gathered, first_expert, experts, capacity):
    group, height, model_dim = gathered.shape
    step = 4
    rows = jax.ShapeDtypeStruct((group * capacity, model_dim), BF16)
    out = pl.BlockSpec((step * capacity, model_dim), lambda s: (s, 0))
    return pl.pallas_call(
        functools.partial(dispatch_kernel, capacity),
        grid=(group // step,),
        in_specs=[
            pl.BlockSpec(memory_space=pltpu.SMEM),
            pl.BlockSpec((step, height, model_dim), lambda s: (s, 0, 0)),
        ],
        out_specs=[out] * (2 * experts),
        out_shape=[rows] * (2 * experts),
        compiler_params=pltpu.CompilerParams(vmem_limit_bytes=56 << 20),
        cost_estimate=pl.CostEstimate(
            flops=4 * experts * group * capacity * 128 * model_dim,
            bytes_accessed=gathered.size * 2 + 4 * experts * group * capacity * model_dim,
            transcendentals=0,
        ),
    )(first_expert, gathered)


def grads_kernel(x_ref, scaled_ref, gate_ref, up_ref, down_ref, grads_ref, hidden_ref, pregate_ref, preup_ref, xt, st):
    shards, _, shard_rows, _ = grads_ref.shape

    @pl.when(pl.program_id(0) == 0)
    def _():
        xt[...] = x_ref[...].T
        st[...] = scaled_ref[...].T

    pre_gate = dot(x_ref[...], gate_ref[...])
    pre_up = dot(x_ref[...], up_ref[...])
    grad_hidden = dot(scaled_ref[...], down_ref[...], CONTRACT_LAST)
    s = jax.nn.sigmoid(pre_gate)
    activation = pre_gate * s
    hidden = (activation * pre_up).astype(BF16)
    grad_pregate = (grad_hidden * pre_up * (s * (1.0 + pre_gate * (1.0 - s)))).astype(BF16)
    grad_preup = (grad_hidden * activation).astype(BF16)
    hidden_ref[...] = hidden
    pregate_ref[...] = grad_pregate
    preup_ref[...] = grad_preup
    for which, (left, right) in enumerate(((xt, grad_pregate), (xt, grad_preup), (st, hidden))):
        product = dot(left[...], right).astype(BF16)
        for r in range(shards):
            grads_ref[r, which] = product[r * shard_rows : (r + 1) * shard_rows]


def expert_grads(x, scaled, gate_proj, up_proj, down_proj, e, shards):
    rows, model_dim = x.shape
    hidden_dim = gate_proj.shape[2]
    tile = 256
    whole = pl.BlockSpec((rows, model_dim), lambda f: (0, 0), pipeline_mode=pl.Buffered(1))
    narrow = pl.BlockSpec((rows, tile), lambda f: (0, f))
    return pl.pallas_call(
        grads_kernel,
        grid=(hidden_dim // tile,),
        in_specs=[
            whole,
            whole,
            pl.BlockSpec((None, model_dim, tile), lambda f: (e, 0, f)),
            pl.BlockSpec((None, model_dim, tile), lambda f: (e, 0, f)),
            pl.BlockSpec((None, tile, model_dim), lambda f: (e, f, 0)),
        ],
        out_specs=[
            pl.BlockSpec((shards, 3, model_dim // shards, tile), lambda f: (0, 0, 0, f)),
            narrow,
            narrow,
            narrow,
        ],
        out_shape=[jax.ShapeDtypeStruct((shards, 3, model_dim // shards, hidden_dim), BF16)]
        + [jax.ShapeDtypeStruct((rows, hidden_dim), BF16)] * 3,
        scratch_shapes=[pltpu.VMEM((model_dim, rows), BF16), pltpu.VMEM((model_dim, rows), BF16)],
        compiler_params=pltpu.CompilerParams(vmem_limit_bytes=56 << 20),
        cost_estimate=pl.CostEstimate(
            flops=12 * rows * model_dim * hidden_dim,
            bytes_accessed=4 * rows * model_dim + 12 * model_dim * hidden_dim + 6 * rows * hidden_dim,
            transcendentals=rows * hidden_dim,
        ),
    )(x, scaled, gate_proj, up_proj, down_proj)


def returns_kernel(hidden_ref, pregate_ref, preup_ref, gate_ref, up_ref, down_ref, back_ref):
    group, height, _ = back_ref.shape
    capacity = height // 2
    out = dot(hidden_ref[...], down_ref[...])
    part = dot(pregate_ref[...], gate_ref[...], CONTRACT_LAST) + dot(preup_ref[...], up_ref[...], CONTRACT_LAST)
    for source in range(group):
        rows = slice(source * capacity, (source + 1) * capacity)
        back_ref[source] = jnp.concatenate([out[rows], part[rows]]).astype(BF16)


def expert_returns(hidden, pregate, preup, gate_proj, up_proj, down_proj, e, group):
    rows, hidden_dim = hidden.shape
    model_dim = gate_proj.shape[1]
    capacity = rows // group
    tile = 512
    whole = pl.BlockSpec((rows, hidden_dim), lambda d: (0, 0), pipeline_mode=pl.Buffered(1))
    return pl.pallas_call(
        returns_kernel,
        grid=(model_dim // tile,),
        in_specs=[
            whole,
            whole,
            whole,
            pl.BlockSpec((None, tile, hidden_dim), lambda d: (e, d, 0)),
            pl.BlockSpec((None, tile, hidden_dim), lambda d: (e, d, 0)),
            pl.BlockSpec((None, hidden_dim, tile), lambda d: (e, 0, d)),
        ],
        out_specs=pl.BlockSpec((group, 2 * capacity, tile), lambda d: (0, 0, d)),
        out_shape=jax.ShapeDtypeStruct((group, 2 * capacity, model_dim), BF16),
        compiler_params=pltpu.CompilerParams(vmem_limit_bytes=48 << 20),
        cost_estimate=pl.CostEstimate(
            flops=600 * rows * model_dim * hidden_dim,
            bytes_accessed=4 * rows * model_dim + 6 * model_dim * hidden_dim + 6 * rows * hidden_dim,
            transcendentals=0,
        ),
    )(hidden, pregate, preup, gate_proj, up_proj, down_proj)


def combine_kernel(cotangent_ref, *refs):
    *pairs, combined_ref, tokens_ref, products_ref, total = refs
    experts = len(pairs) // 2
    tok_dev = combined_ref.shape[0]
    devices, height, model_dim = pairs[0].shape
    step = pl.program_id(0)

    @pl.when(step == 0)
    def _():
        total[...] = jnp.zeros_like(total)

    for e in range(experts):
        rows = pairs[2 * e][...].reshape(devices * height, model_dim)
        picks = pairs[2 * e + 1][...]
        total[...] += dot(picks, rows, CONTRACT_FIRST)
        product = dot(rows, cotangent_ref[...], CONTRACT_LAST)
        product = jnp.where(picks[:, :tok_dev].astype(F32) > 0.0, product, 0.0)
        for d in range(devices):
            products_ref[e, d] = jnp.sum(product[d * height : d * height + height // 2], axis=0, keepdims=True)

    @pl.when(step == pl.num_programs(0) - 1)
    def _():
        combined_ref[...] = total[:tok_dev].astype(BF16)
        tokens_ref[...] = total[tok_dev:].astype(BF16)


def combine(cotangent, returned, picks):
    experts = len(returned)
    group, height, model_dim = returned[0].shape
    tok_dev = cotangent.shape[0]
    step = 4
    whole = pl.BlockSpec((tok_dev, model_dim), lambda s: (0, 0))
    return pl.pallas_call(
        combine_kernel,
        grid=(group // step,),
        in_specs=[whole]
        + [
            pl.BlockSpec((step, height, model_dim), lambda s: (s, 0, 0)),
            pl.BlockSpec((step * height, 2 * tok_dev), lambda s: (s, 0)),
        ]
        * experts,
        out_specs=[whole, whole, pl.BlockSpec((experts, step, 1, tok_dev), lambda s: (0, s, 0, 0))],
        out_shape=[
            jax.ShapeDtypeStruct((tok_dev, model_dim), BF16),
            jax.ShapeDtypeStruct((tok_dev, model_dim), BF16),
            jax.ShapeDtypeStruct((experts, group, 1, tok_dev), F32),
        ],
        scratch_shapes=[pltpu.VMEM((2 * tok_dev, model_dim), F32)],
        compiler_params=pltpu.CompilerParams(vmem_limit_bytes=60 << 20),
        cost_estimate=pl.CostEstimate(
            flops=6 * experts * group * height * tok_dev * model_dim,
            bytes_accessed=2 * experts * group * height * (model_dim + 2 * tok_dev),
            transcendentals=0,
        ),
    )(cotangent, *[v for pair in zip(returned, picks) for v in pair])


def place_kernel(*refs):
    *reduced, gate_ref, up_ref, down_ref = refs
    for e, ref in enumerate(reduced):
        gate_ref[e] = ref[0]
        up_ref[e] = ref[1]
        down_ref[e] = ref[2].T


def place_grads(reduced):
    experts = len(reduced)
    _, shard_rows, hidden_dim = reduced[0].shape
    tile = 256
    straight = pl.BlockSpec((experts, shard_rows, tile), lambda f: (0, 0, f))
    return pl.pallas_call(
        place_kernel,
        grid=(hidden_dim // tile,),
        in_specs=[pl.BlockSpec((3, shard_rows, tile), lambda f: (0, 0, f))] * experts,
        out_specs=[straight, straight, pl.BlockSpec((experts, tile, shard_rows), lambda f: (0, f, 0))],
        out_shape=[
            jax.ShapeDtypeStruct((experts, shard_rows, hidden_dim), BF16),
            jax.ShapeDtypeStruct((experts, shard_rows, hidden_dim), BF16),
            jax.ShapeDtypeStruct((experts, hidden_dim, shard_rows), BF16),
        ],
        compiler_params=pltpu.CompilerParams(vmem_limit_bytes=60 << 20),
        cost_estimate=pl.CostEstimate(
            flops=0, bytes_accessed=12 * experts * shard_rows * hidden_dim, transcendentals=0
        ),
    )(*reduced)


def exchange(rows):
    return lax.all_to_all(rows, "expert", split_axis=0, concat_axis=0, tiled=True)


def local(tokens, cotangent, expert_ids, gate_weights, token_counts, gate_proj, up_proj, down_proj):
    group = lax.axis_size("expert")
    shards = lax.axis_size("dp")
    local_experts, model_dim, hidden_dim = gate_proj.shape
    tok_dev, top = expert_ids.shape
    experts_total = group * local_experts
    capacity = 3 * tok_dev * top // (2 * experts_total)

    live = lax.broadcasted_iota(jnp.int32, (tok_dev, top), 0) < token_counts[0]
    named = jnp.where(live, expert_ids, NOBODY)
    routing = jnp.concatenate([named.T.astype(BF16), gate_weights.T])
    routing = jnp.pad(routing, ((0, 0), (0, model_dim - tok_dev)))
    gathered = lax.all_gather(
        jnp.concatenate([tokens, cotangent, routing])[None], "expert", axis=0, tiled=True
    )

    labels = lax.broadcasted_iota(jnp.int32, (experts_total, 1, 1), 0)
    hits = named.T[None] == labels
    names = jnp.any(hits, axis=1)
    gates = jnp.sum(jnp.where(hits, gate_weights.T[None].astype(F32), 0.0), axis=1)
    before = (
        lax.broadcasted_iota(jnp.int32, (tok_dev, tok_dev), 0)
        < lax.broadcasted_iota(jnp.int32, (tok_dev, tok_dev), 1)
    )
    rank = dot(names.astype(BF16), before.astype(BF16)).astype(jnp.int32)
    names, gates, rank = (v.reshape(group, local_experts, 1, tok_dev) for v in (names, gates, rank))
    column = lax.broadcasted_iota(jnp.int32, (1, 2 * capacity, 1), 1)
    picks = []
    for e in range(local_experts):
        place = names[:, e] & (rank[:, e] == column)
        second = names[:, e] & (rank[:, e] + capacity == column)
        picks.append(
            jnp.concatenate([jnp.where(place, gates[:, e], 0.0).astype(BF16), second.astype(BF16)], axis=2)
            .reshape(-1, 2 * tok_dev)
        )

    gathered, *picks = lax.optimization_barrier((gathered, *picks))
    first = (lax.axis_index("expert") * local_experts).astype(jnp.int32).reshape(1)
    picked = dispatch(gathered, first, local_experts, capacity)

    returned, reduced = [], []
    for e in range(local_experts):
        grads, hidden, pregate, preup = expert_grads(
            picked[2 * e], picked[2 * e + 1], gate_proj, up_proj, down_proj, e, shards
        )
        reduced.append(lax.psum_scatter(grads, "dp", scatter_dimension=0, tiled=False))
        back = expert_returns(hidden, pregate, preup, gate_proj, up_proj, down_proj, e, group)
        returned.append(exchange(back))

    combined, tokens_grad, products = combine(cotangent, returned, picks)
    per_expert = products.transpose(1, 0, 2, 3).reshape(experts_total, 1, tok_dev)
    gates_grad = jnp.sum(jnp.where(hits, per_expert, 0.0), axis=0).T
    return (
        combined,
        tokens_grad,
        gates_grad.astype(BF16),
        *place_grads(reduced),
    )


def solution(mesh):
    both = ("dp", "expert")
    return jax.shard_map(
        local,
        mesh=mesh,
        in_specs=(
            P(both, None),
            P(both, None),
            P(both, None),
            P(both, None),
            P(both),
            P("expert", None, None),
            P("expert", None, None),
            P("expert", None, None),
        ),
        out_specs=(
            P(both, None),
            P(both, None),
            P(both, None),
            P("expert", "dp", None),
            P("expert", "dp", None),
            P("expert", None, "dp"),
        ),
        check_vma=False,
    )
```

```python
import functools

import jax
import jax.numpy as jnp
from jax import lax
from jax.experimental import pallas as pl
from jax.experimental.pallas import tpu as pltpu
from jax.sharding import PartitionSpec as P

F32 = jnp.float32
BF16 = jnp.bfloat16
CONTRACT_FIRST = (((0,), (0,)), ((), ()))
CONTRACT_LAST = (((1,), (1,)), ((), ()))
NOBODY = -1


def dot(a, b, dims=(((1,), (0,)), ((), ()))):
    return lax.dot_general(a, b, dims, preferred_element_type=F32)


def grads_kernel(
    steps,
    first_ref,
    block_ref,
    gate_ref,
    up_ref,
    down_ref,
    grads_ref,
    hidden_ref,
    pregate_ref,
    preup_ref,
    x,
    xt,
    sc,
    st,
):
    step = pl.program_id(0)
    sources = block_ref.shape[0]
    tok_dev = 128
    rows, model_dim = x.shape
    capacity = rows // (steps * sources)
    shards, _, shard_rows, _ = grads_ref.shape

    @pl.when(step < steps)
    def _():
        before = (
            lax.broadcasted_iota(jnp.int32, (tok_dev, tok_dev), 0)
            < lax.broadcasted_iota(jnp.int32, (tok_dev, tok_dev), 1)
        ).astype(BF16)
        column = lax.broadcasted_iota(jnp.int32, (capacity, tok_dev), 0).astype(F32)
        expert = first_ref[0].astype(F32)
        names, gates = [], []
        for j in range(sources):
            routing = block_ref[j, 2 * tok_dev :, :tok_dev].astype(F32)
            hit = routing[:8] == expert
            names.append(jnp.max(jnp.where(hit, 1.0, 0.0), axis=0, keepdims=True))
            gates.append(jnp.sum(jnp.where(hit, routing[8:], 0.0), axis=0, keepdims=True))
        names = jnp.concatenate(names + [jnp.zeros((8 - sources, tok_dev), F32)])
        ranks = dot(names.astype(BF16), before)
        picked = []
        none = jnp.zeros((capacity, tok_dev), F32)
        for j in range(sources):
            here = (ranks[j : j + 1] == column) & (names[j : j + 1] > 0.0)
            place = jnp.concatenate([jnp.where(here, 1.0, 0.0), none], axis=1)
            weight = jnp.concatenate([none, jnp.where(here, gates[j], 0.0)], axis=1)
            picks = jnp.concatenate([place, weight]).astype(BF16)
            picked.append(dot(picks, block_ref[j, : 2 * tok_dev, :]))
        span = pl.ds(pl.multiple_of(step * sources * capacity, sources * capacity), sources * capacity)
        x[span, :] = jnp.concatenate([pair[:capacity] for pair in picked]).astype(BF16)
        sc[span, :] = jnp.concatenate([pair[capacity:] for pair in picked]).astype(BF16)

    for part in range(2):
        span = slice(part * rows // 2, (part + 1) * rows // 2)

        @pl.when(step == (part + 1) * steps // 2 - 1)
        def _():
            xt[:, span] = x[span, :].T
            st[:, span] = sc[span, :].T

    @pl.when(step >= steps)
    def _():
        pre_gate = dot(x[...], gate_ref[...])
        pre_up = dot(x[...], up_ref[...])
        grad_hidden = dot(sc[...], down_ref[...], CONTRACT_LAST)
        s = jax.nn.sigmoid(pre_gate)
        activation = pre_gate * s
        hidden = (activation * pre_up).astype(BF16)
        grad_pregate = (grad_hidden * pre_up * (s * (1.0 + pre_gate * (1.0 - s)))).astype(BF16)
        grad_preup = (grad_hidden * activation).astype(BF16)
        hidden_ref[...] = hidden
        pregate_ref[...] = grad_pregate
        preup_ref[...] = grad_preup
        for which, (left, right) in enumerate(((xt, grad_pregate), (xt, grad_preup), (st, hidden))):
            product = dot(left[...], right).astype(BF16)
            for r in range(shards):
                grads_ref[r, which] = product[r * shard_rows : (r + 1) * shard_rows]


def expert_grads(gathered, expert, gate_proj, up_proj, down_proj, e, capacity, shards):
    group, height, model_dim = gathered.shape
    rows = group * capacity
    hidden_dim = gate_proj.shape[2]
    tile = 256
    sources = 4
    steps = group // sources

    def at(s):
        return jnp.maximum(s - steps, 0)

    narrow = pl.BlockSpec((rows, tile), lambda s: (0, at(s)))
    return pl.pallas_call(
        functools.partial(grads_kernel, steps),
        grid=(steps + hidden_dim // tile,),
        in_specs=[
            pl.BlockSpec(memory_space=pltpu.SMEM),
            pl.BlockSpec((sources, height, model_dim), lambda s: (jnp.minimum(s, steps - 1), 0, 0)),
            pl.BlockSpec((None, model_dim, tile), lambda s: (e, 0, at(s))),
            pl.BlockSpec((None, model_dim, tile), lambda s: (e, 0, at(s))),
            pl.BlockSpec((None, tile, model_dim), lambda s: (e, at(s), 0)),
        ],
        out_specs=[
            pl.BlockSpec((shards, 3, model_dim // shards, tile), lambda s: (0, 0, 0, at(s))),
            narrow,
            narrow,
            narrow,
        ],
        out_shape=[jax.ShapeDtypeStruct((shards, 3, model_dim // shards, hidden_dim), BF16)]
        + [jax.ShapeDtypeStruct((rows, hidden_dim), BF16)] * 3,
        scratch_shapes=[pltpu.VMEM((rows, model_dim), BF16), pltpu.VMEM((model_dim, rows), BF16)] * 2,
        compiler_params=pltpu.CompilerParams(vmem_limit_bytes=60 << 20),
        cost_estimate=pl.CostEstimate(
            flops=12 * rows * model_dim * hidden_dim,
            bytes_accessed=2 * gathered.size + 12 * model_dim * hidden_dim + 6 * rows * hidden_dim,
            transcendentals=rows * hidden_dim,
        ),
    )(expert, gathered, gate_proj, up_proj, down_proj)


def returns_kernel(hidden_ref, pregate_ref, preup_ref, gate_ref, up_ref, down_ref, back_ref):
    group, height, _ = back_ref.shape
    capacity = height // 2
    out = dot(hidden_ref[...], down_ref[...])
    part = dot(pregate_ref[...], gate_ref[...], CONTRACT_LAST) + dot(preup_ref[...], up_ref[...], CONTRACT_LAST)
    for source in range(group):
        rows = slice(source * capacity, (source + 1) * capacity)
        back_ref[source] = jnp.concatenate([out[rows], part[rows]]).astype(BF16)


def expert_returns(hidden, pregate, preup, gate_proj, up_proj, down_proj, e, group):
    rows, hidden_dim = hidden.shape
    model_dim = gate_proj.shape[1]
    capacity = rows // group
    tile = 512
    whole = pl.BlockSpec((rows, hidden_dim), lambda d: (0, 0), pipeline_mode=pl.Buffered(1))
    return pl.pallas_call(
        returns_kernel,
        grid=(model_dim // tile,),
        in_specs=[
            whole,
            whole,
            whole,
            pl.BlockSpec((None, tile, hidden_dim), lambda d: (e, d, 0)),
            pl.BlockSpec((None, tile, hidden_dim), lambda d: (e, d, 0)),
            pl.BlockSpec((None, hidden_dim, tile), lambda d: (e, 0, d)),
        ],
        out_specs=pl.BlockSpec((group, 2 * capacity, tile), lambda d: (0, 0, d)),
        out_shape=jax.ShapeDtypeStruct((group, 2 * capacity, model_dim), BF16),
        compiler_params=pltpu.CompilerParams(vmem_limit_bytes=60 << 20),
        cost_estimate=pl.CostEstimate(
            flops=600 * rows * model_dim * hidden_dim,
            bytes_accessed=4 * rows * model_dim + 6 * model_dim * hidden_dim + 6 * rows * hidden_dim,
            transcendentals=0,
        ),
    )(hidden, pregate, preup, gate_proj, up_proj, down_proj)


def finish_kernel(experts, cotangent_ref, *refs):
    pairs, reduced = refs[: 2 * experts], refs[2 * experts : 3 * experts]
    combined_ref, tokens_ref, products_ref, gate_ref, up_ref, down_ref, total = refs[3 * experts :]
    tok_dev = combined_ref.shape[0]
    devices, height, model_dim = pairs[0].shape
    step = pl.program_id(0)

    for e in range(experts):
        gate_ref[e] = reduced[e][0]
        up_ref[e] = reduced[e][1]
        down_ref[e] = reduced[e][2].T

    sums = None
    for e in range(experts):
        rows = pairs[2 * e][...].reshape(devices * height, model_dim)
        picks = pairs[2 * e + 1][...]
        part = dot(picks, rows, CONTRACT_FIRST)
        sums = part if sums is None else sums + part
        product = dot(rows, cotangent_ref[...], CONTRACT_LAST)
        product = jnp.where(picks[:, :tok_dev].astype(F32) > 0.0, product, 0.0)
        for d in range(devices):
            products_ref[e, d] = jnp.sum(product[d * height : d * height + height // 2], axis=0, keepdims=True)

    @pl.when(step == 0)
    def _():
        total[...] = sums

    @pl.when(step > 0)
    def _():
        total[...] += sums

    @pl.when(step == pl.num_programs(0) - 1)
    def _():
        combined_ref[...] = total[:tok_dev].astype(BF16)
        tokens_ref[...] = total[tok_dev:].astype(BF16)


def finish(cotangent, returned, picks, reduced):
    experts = len(returned)
    group, height, model_dim = returned[0].shape
    tok_dev = cotangent.shape[0]
    _, shard_rows, hidden_dim = reduced[0].shape
    steps = 2
    step, tile = group // steps, hidden_dim // steps
    whole = pl.BlockSpec((tok_dev, model_dim), lambda s: (0, 0))
    straight = pl.BlockSpec((experts, shard_rows, tile), lambda s: (0, 0, s))
    return pl.pallas_call(
        functools.partial(finish_kernel, experts),
        grid=(steps,),
        in_specs=[whole]
        + [
            pl.BlockSpec((step, height, model_dim), lambda s: (s, 0, 0)),
            pl.BlockSpec((step * height, 2 * tok_dev), lambda s: (s, 0)),
        ]
        * experts
        + [pl.BlockSpec((3, shard_rows, tile), lambda s: (0, 0, s))] * experts,
        out_specs=[
            whole,
            whole,
            pl.BlockSpec((experts, step, 1, tok_dev), lambda s: (0, s, 0, 0)),
            straight,
            straight,
            pl.BlockSpec((experts, tile, shard_rows), lambda s: (0, s, 0)),
        ],
        out_shape=[
            jax.ShapeDtypeStruct((tok_dev, model_dim), BF16),
            jax.ShapeDtypeStruct((tok_dev, model_dim), BF16),
            jax.ShapeDtypeStruct((experts, group, 1, tok_dev), F32),
            jax.ShapeDtypeStruct((experts, shard_rows, hidden_dim), BF16),
            jax.ShapeDtypeStruct((experts, shard_rows, hidden_dim), BF16),
            jax.ShapeDtypeStruct((experts, hidden_dim, shard_rows), BF16),
        ],
        scratch_shapes=[pltpu.VMEM((2 * tok_dev, model_dim), F32)],
        compiler_params=pltpu.CompilerParams(vmem_limit_bytes=60 << 20),
        cost_estimate=pl.CostEstimate(
            flops=6 * experts * group * height * tok_dev * model_dim,
            bytes_accessed=2 * experts * (group * height * (model_dim + 2 * tok_dev) + 6 * shard_rows * hidden_dim),
            transcendentals=0,
        ),
    )(cotangent, *[v for pair in zip(returned, picks) for v in pair], *reduced)


def exchange(rows):
    return lax.all_to_all(rows, "expert", split_axis=0, concat_axis=0, tiled=True)


def local(tokens, cotangent, expert_ids, gate_weights, token_counts, gate_proj, up_proj, down_proj):
    group = lax.axis_size("expert")
    shards = lax.axis_size("dp")
    local_experts, model_dim, hidden_dim = gate_proj.shape
    tok_dev, top = expert_ids.shape
    experts_total = group * local_experts
    capacity = 3 * tok_dev * top // (2 * experts_total)

    live = lax.broadcasted_iota(jnp.int32, (tok_dev, top), 0) < token_counts[0]
    named = jnp.where(live, expert_ids, NOBODY)
    routing = jnp.concatenate([named.T.astype(BF16), gate_weights.T])
    routing = jnp.pad(routing, ((0, 0), (0, model_dim - tok_dev)))
    gathered = lax.all_gather(
        jnp.concatenate([tokens, cotangent, routing])[None], "expert", axis=0, tiled=True
    )

    labels = lax.broadcasted_iota(jnp.int32, (experts_total, 1, 1), 0)
    hits = named.T[None] == labels
    names = jnp.any(hits, axis=1)
    gates = jnp.sum(jnp.where(hits, gate_weights.T[None].astype(F32), 0.0), axis=1)
    before = (
        lax.broadcasted_iota(jnp.int32, (tok_dev, tok_dev), 0)
        < lax.broadcasted_iota(jnp.int32, (tok_dev, tok_dev), 1)
    )
    rank = dot(names.astype(BF16), before.astype(BF16)).astype(jnp.int32)
    names, gates, rank = (v.reshape(group, local_experts, 1, tok_dev) for v in (names, gates, rank))
    column = lax.broadcasted_iota(jnp.int32, (1, 2 * capacity, 1), 1)
    picks = []
    for e in range(local_experts):
        place = names[:, e] & (rank[:, e] == column)
        second = names[:, e] & (rank[:, e] + capacity == column)
        picks.append(
            jnp.concatenate([jnp.where(place, gates[:, e], 0.0).astype(BF16), second.astype(BF16)], axis=2)
            .reshape(-1, 2 * tok_dev)
        )

    gathered, *picks = lax.optimization_barrier((gathered, *picks))
    first = (lax.axis_index("expert") * local_experts).astype(jnp.int32).reshape(1)

    returned, reduced = [], []
    for e in range(local_experts):
        grads, hidden, pregate, preup = expert_grads(
            gathered, first + e, gate_proj, up_proj, down_proj, e, capacity, shards
        )
        reduced.append(lax.psum_scatter(grads, "dp", scatter_dimension=0, tiled=False))
        back = expert_returns(hidden, pregate, preup, gate_proj, up_proj, down_proj, e, group)
        returned.append(exchange(back))

    combined, tokens_grad, products, *weight_grads = finish(cotangent, returned, picks, reduced)
    per_expert = products.transpose(1, 0, 2, 3).reshape(experts_total, 1, tok_dev)
    gates_grad = jnp.sum(jnp.where(hits, per_expert, 0.0), axis=0).T
    return (
        combined,
        tokens_grad,
        gates_grad.astype(BF16),
        *weight_grads,
    )


def solution(mesh):
    both = ("dp", "expert")
    return jax.shard_map(
        local,
        mesh=mesh,
        in_specs=(
            P(both, None),
            P(both, None),
            P(both, None),
            P(both, None),
            P(both),
            P("expert", None, None),
            P("expert", None, None),
            P("expert", None, None),
        ),
        out_specs=(
            P(both, None),
            P(both, None),
            P(both, None),
            P("expert", "dp", None),
            P("expert", "dp", None),
            P("expert", None, "dp"),
        ),
        check_vma=False,
    )
```

```python
import functools

import jax
import jax.numpy as jnp
from jax import lax
from jax.experimental import pallas as pl
from jax.experimental.pallas import tpu as pltpu
from jax.sharding import PartitionSpec as P

F32 = jnp.float32
BF16 = jnp.bfloat16
CONTRACT_FIRST = (((0,), (0,)), ((), ()))
CONTRACT_LAST = (((1,), (1,)), ((), ()))
NOBODY = -1


def dot(a, b, dims=(((1,), (0,)), ((), ()))):
    return lax.dot_general(a, b, dims, preferred_element_type=F32)


def grads_kernel(steps, sources, e, plan_ref, *refs):
    blocks, (gate_ref, up_ref, down_ref) = refs[:sources], refs[sources : sources + 3]
    grads_ref, hidden_ref, pregate_ref, preup_ref, x, xt, sc, st = refs[sources + 3 :]
    step = pl.program_id(0)
    tok_dev = plan_ref.shape[2]
    rows, model_dim = x.shape
    capacity = rows // (steps * sources)
    shards, _, shard_rows, _ = grads_ref.shape

    @pl.when(step < steps)
    def _():
        column = lax.broadcasted_iota(jnp.int32, (capacity, tok_dev), 0).astype(F32)
        none = jnp.zeros((capacity, tok_dev), F32)
        picked = []
        for j in range(sources):
            here = plan_ref[j, 2 * e : 2 * e + 1, :] == column
            place = jnp.concatenate([jnp.where(here, 1.0, 0.0), none], axis=1)
            weight = jnp.concatenate([none, jnp.where(here, plan_ref[j, 2 * e + 1 : 2 * e + 2, :], 0.0)], axis=1)
            picks = jnp.concatenate([place, weight]).astype(BF16)
            picked.append(dot(picks, blocks[j][...]))
        span = pl.ds(pl.multiple_of(step * sources * capacity, sources * capacity), sources * capacity)
        x[span, :] = jnp.concatenate([pair[:capacity] for pair in picked]).astype(BF16)
        sc[span, :] = jnp.concatenate([pair[capacity:] for pair in picked]).astype(BF16)

    for part in range(2):
        span = slice(part * rows // 2, (part + 1) * rows // 2)

        @pl.when(step == (part + 1) * steps // 2 - 1)
        def _():
            xt[:, span] = x[span, :].T
            st[:, span] = sc[span, :].T

    @pl.when(step >= steps)
    def _():
        pre_gate = dot(x[...], gate_ref[...])
        pre_up = dot(x[...], up_ref[...])
        grad_hidden = dot(sc[...], down_ref[...], CONTRACT_LAST)
        s = jax.nn.sigmoid(pre_gate)
        activation = pre_gate * s
        hidden = (activation * pre_up).astype(BF16)
        grad_pregate = (grad_hidden * pre_up * (s * (1.0 + pre_gate * (1.0 - s)))).astype(BF16)
        grad_preup = (grad_hidden * activation).astype(BF16)
        hidden_ref[...] = hidden
        pregate_ref[...] = grad_pregate
        preup_ref[...] = grad_preup
        for which, (left, right) in enumerate(((xt, grad_pregate), (xt, grad_preup), (st, hidden))):
            product = dot(left[...], right).astype(BF16)
            for r in range(shards):
                grads_ref[r, which] = product[r * shard_rows : (r + 1) * shard_rows]


def expert_grads(gathered, plan, gate_proj, up_proj, down_proj, e, capacity, shards):
    group, height, model_dim = gathered.shape
    rows = group * capacity
    hidden_dim = gate_proj.shape[2]
    tile = 256
    sources = 4
    steps = group // sources

    def at(s):
        return jnp.maximum(s - steps, 0)

    def source(j):
        return lambda s: (jnp.minimum(s, steps - 1) * sources + j, 0, 0)

    narrow = pl.BlockSpec((rows, tile), lambda s: (0, at(s)))
    return pl.pallas_call(
        functools.partial(grads_kernel, steps, sources, e),
        grid=(steps + hidden_dim // tile,),
        in_specs=[
            pl.BlockSpec((sources, *plan.shape[1:]), lambda s: (jnp.minimum(s, steps - 1), 0, 0)),
            *[pl.BlockSpec((None, height, model_dim), source(j)) for j in range(sources)],
            pl.BlockSpec((None, model_dim, tile), lambda s: (e, 0, at(s))),
            pl.BlockSpec((None, model_dim, tile), lambda s: (e, 0, at(s))),
            pl.BlockSpec((None, tile, model_dim), lambda s: (e, at(s), 0)),
        ],
        out_specs=[
            pl.BlockSpec((shards, 3, model_dim // shards, tile), lambda s: (0, 0, 0, at(s))),
            narrow,
            narrow,
            narrow,
        ],
        out_shape=[jax.ShapeDtypeStruct((shards, 3, model_dim // shards, hidden_dim), BF16)]
        + [jax.ShapeDtypeStruct((rows, hidden_dim), BF16)] * 3,
        scratch_shapes=[pltpu.VMEM((rows, model_dim), BF16), pltpu.VMEM((model_dim, rows), BF16)] * 2,
        compiler_params=pltpu.CompilerParams(vmem_limit_bytes=60 << 20),
        cost_estimate=pl.CostEstimate(
            flops=12 * rows * model_dim * hidden_dim,
            bytes_accessed=2 * gathered.size + 12 * model_dim * hidden_dim + 6 * rows * hidden_dim,
            transcendentals=rows * hidden_dim,
        ),
    )(plan, *[gathered] * sources, gate_proj, up_proj, down_proj)


def returns_kernel(hidden_ref, pregate_ref, preup_ref, gate_ref, up_ref, down_ref, back_ref):
    group, height, _ = back_ref.shape
    capacity = height // 2
    out = dot(hidden_ref[...], down_ref[...])
    part = dot(pregate_ref[...], gate_ref[...], CONTRACT_LAST) + dot(preup_ref[...], up_ref[...], CONTRACT_LAST)
    for source in range(group):
        rows = slice(source * capacity, (source + 1) * capacity)
        back_ref[source] = jnp.concatenate([out[rows], part[rows]]).astype(BF16)


def expert_returns(hidden, pregate, preup, gate_proj, up_proj, down_proj, e, group):
    rows, hidden_dim = hidden.shape
    model_dim = gate_proj.shape[1]
    capacity = rows // group
    tile = 512
    whole = pl.BlockSpec((rows, hidden_dim), lambda d: (0, 0), pipeline_mode=pl.Buffered(1))
    return pl.pallas_call(
        returns_kernel,
        grid=(model_dim // tile,),
        in_specs=[
            whole,
            whole,
            whole,
            pl.BlockSpec((None, tile, hidden_dim), lambda d: (e, d, 0)),
            pl.BlockSpec((None, tile, hidden_dim), lambda d: (e, d, 0)),
            pl.BlockSpec((None, hidden_dim, tile), lambda d: (e, 0, d)),
        ],
        out_specs=pl.BlockSpec((group, 2 * capacity, tile), lambda d: (0, 0, d)),
        out_shape=jax.ShapeDtypeStruct((group, 2 * capacity, model_dim), BF16),
        compiler_params=pltpu.CompilerParams(vmem_limit_bytes=60 << 20),
        cost_estimate=pl.CostEstimate(
            flops=600 * rows * model_dim * hidden_dim,
            bytes_accessed=4 * rows * model_dim + 6 * model_dim * hidden_dim + 6 * rows * hidden_dim,
            transcendentals=0,
        ),
    )(hidden, pregate, preup, gate_proj, up_proj, down_proj)


def finish_kernel(experts, cotangent_ref, *refs):
    pairs, reduced = refs[: 2 * experts], refs[2 * experts : 3 * experts]
    combined_ref, tokens_ref, products_ref, gate_ref, up_ref, down_ref, total = refs[3 * experts :]
    tok_dev = combined_ref.shape[0]
    devices, height, model_dim = pairs[0].shape
    step = pl.program_id(0)

    for e in range(experts):
        gate_ref[e] = reduced[e][0]
        up_ref[e] = reduced[e][1]
        down_ref[e] = reduced[e][2].T

    sums = None
    for e in range(experts):
        rows = pairs[2 * e][...].reshape(devices * height, model_dim)
        picks = pairs[2 * e + 1][...]
        part = dot(picks, rows, CONTRACT_FIRST)
        sums = part if sums is None else sums + part
        product = dot(rows, cotangent_ref[...], CONTRACT_LAST)
        product = jnp.where(picks[:, :tok_dev].astype(F32) > 0.0, product, 0.0)
        for d in range(devices):
            products_ref[e, d] = jnp.sum(product[d * height : d * height + height // 2], axis=0, keepdims=True)

    @pl.when(step == 0)
    def _():
        total[...] = sums

    @pl.when(step > 0)
    def _():
        total[...] += sums

    @pl.when(step == pl.num_programs(0) - 1)
    def _():
        combined_ref[...] = total[:tok_dev].astype(BF16)
        tokens_ref[...] = total[tok_dev:].astype(BF16)


def finish(cotangent, returned, picks, reduced):
    experts = len(returned)
    group, height, model_dim = returned[0].shape
    tok_dev = cotangent.shape[0]
    _, shard_rows, hidden_dim = reduced[0].shape
    steps = 2
    step, tile = group // steps, hidden_dim // steps
    whole = pl.BlockSpec((tok_dev, model_dim), lambda s: (0, 0))
    straight = pl.BlockSpec((experts, shard_rows, tile), lambda s: (0, 0, s))
    return pl.pallas_call(
        functools.partial(finish_kernel, experts),
        grid=(steps,),
        in_specs=[whole]
        + [
            pl.BlockSpec((step, height, model_dim), lambda s: (s, 0, 0)),
            pl.BlockSpec((step * height, 2 * tok_dev), lambda s: (s, 0)),
        ]
        * experts
        + [pl.BlockSpec((3, shard_rows, tile), lambda s: (0, 0, s))] * experts,
        out_specs=[
            whole,
            whole,
            pl.BlockSpec((experts, step, 1, tok_dev), lambda s: (0, s, 0, 0)),
            straight,
            straight,
            pl.BlockSpec((experts, tile, shard_rows), lambda s: (0, s, 0)),
        ],
        out_shape=[
            jax.ShapeDtypeStruct((tok_dev, model_dim), BF16),
            jax.ShapeDtypeStruct((tok_dev, model_dim), BF16),
            jax.ShapeDtypeStruct((experts, group, 1, tok_dev), F32),
            jax.ShapeDtypeStruct((experts, shard_rows, hidden_dim), BF16),
            jax.ShapeDtypeStruct((experts, shard_rows, hidden_dim), BF16),
            jax.ShapeDtypeStruct((experts, hidden_dim, shard_rows), BF16),
        ],
        scratch_shapes=[pltpu.VMEM((2 * tok_dev, model_dim), F32)],
        compiler_params=pltpu.CompilerParams(vmem_limit_bytes=60 << 20),
        cost_estimate=pl.CostEstimate(
            flops=6 * experts * group * height * tok_dev * model_dim,
            bytes_accessed=2 * experts * (group * height * (model_dim + 2 * tok_dev) + 6 * shard_rows * hidden_dim),
            transcendentals=0,
        ),
    )(cotangent, *[v for pair in zip(returned, picks) for v in pair], *reduced)


def exchange(rows):
    return lax.all_to_all(rows, "expert", split_axis=0, concat_axis=0, tiled=True)


def local(tokens, cotangent, expert_ids, gate_weights, token_counts, gate_proj, up_proj, down_proj):
    group = lax.axis_size("expert")
    shards = lax.axis_size("dp")
    local_experts, model_dim, hidden_dim = gate_proj.shape
    tok_dev, top = expert_ids.shape
    experts_total = group * local_experts
    capacity = 3 * tok_dev * top // (2 * experts_total)

    live = lax.broadcasted_iota(jnp.int32, (tok_dev, top), 0) < token_counts[0]
    named = jnp.where(live, expert_ids, NOBODY)
    gathered = lax.all_gather(jnp.concatenate([tokens, cotangent])[None], "expert", axis=0, tiled=True)

    labels = lax.broadcasted_iota(jnp.int32, (experts_total, 1, 1), 0)
    hits = named.T[None] == labels
    names = jnp.any(hits, axis=1)
    gates = jnp.sum(jnp.where(hits, gate_weights.T[None].astype(F32), 0.0), axis=1)
    before = (
        lax.broadcasted_iota(jnp.int32, (tok_dev, tok_dev), 0)
        < lax.broadcasted_iota(jnp.int32, (tok_dev, tok_dev), 1)
    )
    rank = dot(names.astype(BF16), before.astype(BF16)).astype(jnp.int32)
    names, gates, rank = (v.reshape(group, local_experts, 1, tok_dev) for v in (names, gates, rank))
    column = lax.broadcasted_iota(jnp.int32, (1, 2 * capacity, 1), 1)
    picks = []
    for e in range(local_experts):
        place = names[:, e] & (rank[:, e] == column)
        second = names[:, e] & (rank[:, e] + capacity == column)
        picks.append(
            jnp.concatenate([jnp.where(place, gates[:, e], 0.0).astype(BF16), second.astype(BF16)], axis=2)
            .reshape(-1, 2 * tok_dev)
        )

    slots = jnp.where(names, rank.astype(F32), -1.0)
    plan = jnp.concatenate([slots, gates], axis=2).reshape(group, 2 * local_experts, tok_dev)
    plan = exchange(jnp.pad(plan, ((0, 0), (0, 8 - 2 * local_experts), (0, 0))))
    gathered, plan, *picks = lax.optimization_barrier((gathered, plan, *picks))

    returned, reduced = [], []
    for e in range(local_experts):
        grads, hidden, pregate, preup = expert_grads(
            gathered, plan, gate_proj, up_proj, down_proj, e, capacity, shards
        )
        reduced.append(lax.psum_scatter(grads, "dp", scatter_dimension=0, tiled=False))
        back = expert_returns(hidden, pregate, preup, gate_proj, up_proj, down_proj, e, group)
        returned.append(exchange(back))

    combined, tokens_grad, products, *weight_grads = finish(cotangent, returned, picks, reduced)
    per_expert = products.transpose(1, 0, 2, 3).reshape(experts_total, 1, tok_dev)
    gates_grad = jnp.sum(jnp.where(hits, per_expert, 0.0), axis=0).T
    return (
        combined,
        tokens_grad,
        gates_grad.astype(BF16),
        *weight_grads,
    )


def solution(mesh):
    both = ("dp", "expert")
    return jax.shard_map(
        local,
        mesh=mesh,
        in_specs=(
            P(both, None),
            P(both, None),
            P(both, None),
            P(both, None),
            P(both),
            P("expert", None, None),
            P("expert", None, None),
            P("expert", None, None),
        ),
        out_specs=(
            P(both, None),
            P(both, None),
            P(both, None),
            P("expert", "dp", None),
            P("expert", "dp", None),
            P("expert", None, "dp"),
        ),
        check_vma=False,
    )
```

```python
import functools

import jax
import jax.numpy as jnp
from jax import lax
from jax.experimental import pallas as pl
from jax.experimental.pallas import tpu as pltpu
from jax.sharding import PartitionSpec as P

F32 = jnp.float32
BF16 = jnp.bfloat16
CONTRACT_FIRST = (((0,), (0,)), ((), ()))
CONTRACT_LAST = (((1,), (1,)), ((), ()))
NOBODY = -1


def dot(a, b, dims=(((1,), (0,)), ((), ()))):
    return lax.dot_general(a, b, dims, preferred_element_type=F32)


def grads_kernel(steps, sources, e, last, plan_ref, *refs):
    blocks, (gate_ref, up_ref, down_ref), refs = refs[:sources], refs[sources : sources + 3], refs[sources + 3 :]
    if last:
        old_hidden_ref, old_scaled_ref, grads_ref, hidden_ref, pregate_ref, preup_ref, x, xt, sc, st, old_st = refs
    else:
        grads_ref, hidden_ref, pregate_ref, preup_ref, scaled_ref, x, xt, sc, sem = refs
        keep = pltpu.make_async_copy(sc, scaled_ref, sem)
    step = pl.program_id(0)
    tok_dev = plan_ref.shape[2]
    rows, model_dim = x.shape
    capacity = rows // (steps * sources)
    shards, _, shard_rows, _ = grads_ref.shape

    @pl.when(step < steps)
    def _():
        column = lax.broadcasted_iota(jnp.int32, (capacity, tok_dev), 0).astype(F32)
        none = jnp.zeros((capacity, tok_dev), F32)
        picked = []
        for j in range(sources):
            here = plan_ref[j, 2 * e : 2 * e + 1, :] == column
            place = jnp.concatenate([jnp.where(here, 1.0, 0.0), none], axis=1)
            weight = jnp.concatenate([none, jnp.where(here, plan_ref[j, 2 * e + 1 : 2 * e + 2, :], 0.0)], axis=1)
            picks = jnp.concatenate([place, weight]).astype(BF16)
            picked.append(dot(picks, blocks[j][...]))
        span = pl.ds(pl.multiple_of(step * sources * capacity, sources * capacity), sources * capacity)
        x[span, :] = jnp.concatenate([pair[:capacity] for pair in picked]).astype(BF16)
        sc[span, :] = jnp.concatenate([pair[capacity:] for pair in picked]).astype(BF16)

    for part in range(2):
        span = slice(part * rows // 2, (part + 1) * rows // 2)

        @pl.when(step == (part + 1) * steps // 2 - 1)
        def _():
            xt[:, span] = x[span, :].T
            if last:
                st[:, span] = sc[span, :].T
                old_st[:, span] = old_scaled_ref[span, :].T

    if not last:

        @pl.when(step == steps)
        def _():
            keep.start()

    @pl.when(step >= steps)
    def _():
        pre_gate = dot(x[...], gate_ref[...])
        pre_up = dot(x[...], up_ref[...])
        grad_hidden = dot(sc[...], down_ref[...], CONTRACT_LAST)
        s = jax.nn.sigmoid(pre_gate)
        activation = pre_gate * s
        hidden = (activation * pre_up).astype(BF16)
        grad_pregate = (grad_hidden * pre_up * (s * (1.0 + pre_gate * (1.0 - s)))).astype(BF16)
        grad_preup = (grad_hidden * activation).astype(BF16)
        hidden_ref[...] = hidden
        pregate_ref[...] = grad_pregate
        preup_ref[...] = grad_preup
        pairs = [(xt, grad_pregate), (xt, grad_preup)]
        if last:
            pairs += [(st, hidden), (old_st, old_hidden_ref[...])]
        for which, (left, right) in enumerate(pairs):
            product = dot(left[...], right).astype(BF16)
            for r in range(shards):
                grads_ref[r, which] = product[r * shard_rows : (r + 1) * shard_rows]

    if not last:

        @pl.when(step == pl.num_programs(0) - 1)
        def _():
            keep.wait()


def expert_grads(gathered, plan, gate_proj, up_proj, down_proj, e, capacity, shards, old):
    group, height, model_dim = gathered.shape
    rows = group * capacity
    hidden_dim = gate_proj.shape[2]
    tile = 256
    sources = 4
    steps = group // sources

    def at(s):
        return jnp.maximum(s - steps, 0)

    def source(j):
        return lambda s: (jnp.minimum(s, steps - 1) * sources + j, 0, 0)

    narrow = pl.BlockSpec((rows, tile), lambda s: (0, at(s)))
    last = old is not None
    matrices = 4 if last else 2
    wide = pltpu.VMEM((rows, model_dim), BF16)
    tall = pltpu.VMEM((model_dim, rows), BF16)
    return pl.pallas_call(
        functools.partial(grads_kernel, steps, sources, e, last),
        grid=(steps + hidden_dim // tile,),
        in_specs=[
            pl.BlockSpec((sources, *plan.shape[1:]), lambda s: (jnp.minimum(s, steps - 1), 0, 0)),
            *[pl.BlockSpec((None, height, model_dim), source(j)) for j in range(sources)],
            pl.BlockSpec((None, model_dim, tile), lambda s: (e, 0, at(s))),
            pl.BlockSpec((None, model_dim, tile), lambda s: (e, 0, at(s))),
            pl.BlockSpec((None, tile, model_dim), lambda s: (e, at(s), 0)),
        ]
        + [narrow, pl.BlockSpec((rows, model_dim), lambda s: (0, 0), pipeline_mode=pl.Buffered(1))] * last,
        out_specs=[
            pl.BlockSpec((shards, matrices, model_dim // shards, tile), lambda s: (0, 0, 0, at(s))),
            narrow,
            narrow,
            narrow,
        ]
        + [pl.BlockSpec(memory_space=pl.ANY)] * (not last),
        out_shape=[jax.ShapeDtypeStruct((shards, matrices, model_dim // shards, hidden_dim), BF16)]
        + [jax.ShapeDtypeStruct((rows, hidden_dim), BF16)] * 3
        + [jax.ShapeDtypeStruct((rows, model_dim), BF16)] * (not last),
        scratch_shapes=[wide, tall, wide] + ([tall, tall] if last else [pltpu.SemaphoreType.DMA]),
        compiler_params=pltpu.CompilerParams(vmem_limit_bytes=61 << 20),
        cost_estimate=pl.CostEstimate(
            flops=12 * rows * model_dim * hidden_dim,
            bytes_accessed=2 * gathered.size + 12 * model_dim * hidden_dim + 6 * rows * hidden_dim,
            transcendentals=rows * hidden_dim,
        ),
    )(plan, *[gathered] * sources, gate_proj, up_proj, down_proj, *(old if last else ()))


def returns_kernel(hidden_ref, pregate_ref, preup_ref, gate_ref, up_ref, down_ref, back_ref):
    group, height, _ = back_ref.shape
    capacity = height // 2
    out = dot(hidden_ref[...], down_ref[...])
    part = dot(pregate_ref[...], gate_ref[...], CONTRACT_LAST) + dot(preup_ref[...], up_ref[...], CONTRACT_LAST)
    for source in range(group):
        rows = slice(source * capacity, (source + 1) * capacity)
        back_ref[source] = jnp.concatenate([out[rows], part[rows]]).astype(BF16)


def expert_returns(hidden, pregate, preup, gate_proj, up_proj, down_proj, e, group):
    rows, hidden_dim = hidden.shape
    model_dim = gate_proj.shape[1]
    capacity = rows // group
    tile = 512
    whole = pl.BlockSpec((rows, hidden_dim), lambda d: (0, 0), pipeline_mode=pl.Buffered(1))
    return pl.pallas_call(
        returns_kernel,
        grid=(model_dim // tile,),
        in_specs=[
            whole,
            whole,
            whole,
            pl.BlockSpec((None, tile, hidden_dim), lambda d: (e, d, 0)),
            pl.BlockSpec((None, tile, hidden_dim), lambda d: (e, d, 0)),
            pl.BlockSpec((None, hidden_dim, tile), lambda d: (e, 0, d)),
        ],
        out_specs=pl.BlockSpec((group, 2 * capacity, tile), lambda d: (0, 0, d)),
        out_shape=jax.ShapeDtypeStruct((group, 2 * capacity, model_dim), BF16),
        compiler_params=pltpu.CompilerParams(vmem_limit_bytes=60 << 20),
        cost_estimate=pl.CostEstimate(
            flops=600 * rows * model_dim * hidden_dim,
            bytes_accessed=4 * rows * model_dim + 6 * model_dim * hidden_dim + 6 * rows * hidden_dim,
            transcendentals=0,
        ),
    )(hidden, pregate, preup, gate_proj, up_proj, down_proj)


def finish_kernel(experts, cotangent_ref, *refs):
    pairs, reduced = refs[: 2 * experts], refs[2 * experts : 3 * experts]
    combined_ref, tokens_ref, products_ref, gate_ref, up_ref, down_ref, total = refs[3 * experts :]
    tok_dev = combined_ref.shape[0]
    devices, height, model_dim = pairs[0].shape
    step = pl.program_id(0)

    for e in range(experts):
        gate_ref[e] = reduced[e][0]
        up_ref[e] = reduced[e][1]
    down_ref[0] = reduced[1][3].T
    down_ref[1] = reduced[1][2].T

    sums = None
    for e in range(experts):
        rows = pairs[2 * e][...].reshape(devices * height, model_dim)
        picks = pairs[2 * e + 1][...]
        part = dot(picks, rows, CONTRACT_FIRST)
        sums = part if sums is None else sums + part
        product = dot(rows, cotangent_ref[...], CONTRACT_LAST)
        product = jnp.where(picks[:, :tok_dev].astype(F32) > 0.0, product, 0.0)
        for d in range(devices):
            products_ref[e, d] = jnp.sum(product[d * height : d * height + height // 2], axis=0, keepdims=True)

    @pl.when(step == 0)
    def _():
        total[...] = sums

    @pl.when(step > 0)
    def _():
        total[...] += sums

    @pl.when(step == pl.num_programs(0) - 1)
    def _():
        combined_ref[...] = total[:tok_dev].astype(BF16)
        tokens_ref[...] = total[tok_dev:].astype(BF16)


def finish(cotangent, returned, picks, reduced):
    experts = len(returned)
    group, height, model_dim = returned[0].shape
    tok_dev = cotangent.shape[0]
    _, shard_rows, hidden_dim = reduced[0].shape
    steps = 2
    step, tile = group // steps, hidden_dim // steps
    whole = pl.BlockSpec((tok_dev, model_dim), lambda s: (0, 0))
    straight = pl.BlockSpec((experts, shard_rows, tile), lambda s: (0, 0, s))
    return pl.pallas_call(
        functools.partial(finish_kernel, experts),
        grid=(steps,),
        in_specs=[whole]
        + [
            pl.BlockSpec((step, height, model_dim), lambda s: (s, 0, 0)),
            pl.BlockSpec((step * height, 2 * tok_dev), lambda s: (s, 0)),
        ]
        * experts
        + [pl.BlockSpec((v.shape[0], shard_rows, tile), lambda s: (0, 0, s)) for v in reduced],
        out_specs=[
            whole,
            whole,
            pl.BlockSpec((experts, step, 1, tok_dev), lambda s: (0, s, 0, 0)),
            straight,
            straight,
            pl.BlockSpec((experts, tile, shard_rows), lambda s: (0, s, 0)),
        ],
        out_shape=[
            jax.ShapeDtypeStruct((tok_dev, model_dim), BF16),
            jax.ShapeDtypeStruct((tok_dev, model_dim), BF16),
            jax.ShapeDtypeStruct((experts, group, 1, tok_dev), F32),
            jax.ShapeDtypeStruct((experts, shard_rows, hidden_dim), BF16),
            jax.ShapeDtypeStruct((experts, shard_rows, hidden_dim), BF16),
            jax.ShapeDtypeStruct((experts, hidden_dim, shard_rows), BF16),
        ],
        scratch_shapes=[pltpu.VMEM((2 * tok_dev, model_dim), F32)],
        compiler_params=pltpu.CompilerParams(vmem_limit_bytes=60 << 20),
        cost_estimate=pl.CostEstimate(
            flops=6 * experts * group * height * tok_dev * model_dim,
            bytes_accessed=2 * experts * (group * height * (model_dim + 2 * tok_dev) + 6 * shard_rows * hidden_dim),
            transcendentals=0,
        ),
    )(cotangent, *[v for pair in zip(returned, picks) for v in pair], *reduced)


def exchange(rows):
    return lax.all_to_all(rows, "expert", split_axis=0, concat_axis=0, tiled=True)


def local(tokens, cotangent, expert_ids, gate_weights, token_counts, gate_proj, up_proj, down_proj):
    group = lax.axis_size("expert")
    shards = lax.axis_size("dp")
    local_experts, model_dim, hidden_dim = gate_proj.shape
    tok_dev, top = expert_ids.shape
    experts_total = group * local_experts
    capacity = 3 * tok_dev * top // (2 * experts_total)

    live = lax.broadcasted_iota(jnp.int32, (tok_dev, top), 0) < token_counts[0]
    named = jnp.where(live, expert_ids, NOBODY)
    gathered = lax.all_gather(jnp.concatenate([tokens, cotangent])[None], "expert", axis=0, tiled=True)

    labels = lax.broadcasted_iota(jnp.int32, (experts_total, 1, 1), 0)
    hits = named.T[None] == labels
    names = jnp.any(hits, axis=1)
    gates = jnp.sum(jnp.where(hits, gate_weights.T[None].astype(F32), 0.0), axis=1)
    before = (
        lax.broadcasted_iota(jnp.int32, (tok_dev, tok_dev), 0)
        < lax.broadcasted_iota(jnp.int32, (tok_dev, tok_dev), 1)
    )
    rank = dot(names.astype(BF16), before.astype(BF16)).astype(jnp.int32)
    names, gates, rank = (v.reshape(group, local_experts, 1, tok_dev) for v in (names, gates, rank))
    column = lax.broadcasted_iota(jnp.int32, (1, 2 * capacity, 1), 1)
    picks = []
    for e in range(local_experts):
        place = names[:, e] & (rank[:, e] == column)
        second = names[:, e] & (rank[:, e] + capacity == column)
        picks.append(
            jnp.concatenate([jnp.where(place, gates[:, e], 0.0).astype(BF16), second.astype(BF16)], axis=2)
            .reshape(-1, 2 * tok_dev)
        )

    slots = jnp.where(names, rank.astype(F32), -1.0)
    plan = jnp.concatenate([slots, gates], axis=2).reshape(group, 2 * local_experts, tok_dev)
    plan = exchange(jnp.pad(plan, ((0, 0), (0, 8 - 2 * local_experts), (0, 0))))
    gathered, plan, *picks = lax.optimization_barrier((gathered, plan, *picks))
    old = None

    returned, reduced = [], []
    for e in range(local_experts):
        grads, hidden, pregate, preup, *scaled = expert_grads(
            gathered, plan, gate_proj, up_proj, down_proj, e, capacity, shards, old
        )
        old = (hidden, *scaled)
        reduced.append(lax.psum_scatter(grads, "dp", scatter_dimension=0, tiled=False))
        back = expert_returns(hidden, pregate, preup, gate_proj, up_proj, down_proj, e, group)
        returned.append(exchange(back))

    combined, tokens_grad, products, *weight_grads = finish(cotangent, returned, picks, reduced)
    per_expert = products.transpose(1, 0, 2, 3).reshape(experts_total, 1, tok_dev)
    gates_grad = jnp.sum(jnp.where(hits, per_expert, 0.0), axis=0).T
    return (
        combined,
        tokens_grad,
        gates_grad.astype(BF16),
        *weight_grads,
    )


def solution(mesh):
    both = ("dp", "expert")
    return jax.shard_map(
        local,
        mesh=mesh,
        in_specs=(
            P(both, None),
            P(both, None),
            P(both, None),
            P(both, None),
            P(both),
            P("expert", None, None),
            P("expert", None, None),
            P("expert", None, None),
        ),
        out_specs=(
            P(both, None),
            P(both, None),
            P(both, None),
            P("expert", "dp", None),
            P("expert", "dp", None),
            P("expert", None, "dp"),
        ),
        check_vma=False,
    )
```

```python
import functools

import jax
import jax.numpy as jnp
from jax import lax
from jax.experimental import pallas as pl
from jax.experimental.pallas import tpu as pltpu
from jax.sharding import PartitionSpec as P

F32 = jnp.float32
BF16 = jnp.bfloat16
CONTRACT_FIRST = (((0,), (0,)), ((), ()))
CONTRACT_LAST = (((1,), (1,)), ((), ()))
NOBODY = -1


def dot(a, b, dims=(((1,), (0,)), ((), ()))):
    return lax.dot_general(a, b, dims, preferred_element_type=F32)


def grads_kernel(steps, sources, e, last, plan_ref, *refs):
    blocks, (gate_ref, up_ref, down_ref), refs = refs[:sources], refs[sources : sources + 3], refs[sources + 3 :]
    if last:
        old_hidden_ref, old_scaled_ref, grads_ref, hidden_ref, pregate_ref, preup_ref, x, xt, sc, st, old_st = refs
    else:
        grads_ref, hidden_ref, pregate_ref, preup_ref, scaled_ref, x, xt, sc, sem = refs
        keep = pltpu.make_async_copy(sc, scaled_ref, sem)
    step = pl.program_id(0)
    tok_dev = plan_ref.shape[2]
    rows, model_dim = x.shape
    capacity = rows // (steps * sources)
    shards, _, shard_rows, _ = grads_ref.shape

    @pl.when(step < steps)
    def _():
        column = lax.broadcasted_iota(jnp.int32, (capacity, tok_dev), 0).astype(F32)
        none = jnp.zeros((capacity, tok_dev), F32)
        picked = []
        for j in range(sources):
            here = plan_ref[j, 2 * e : 2 * e + 1, :] == column
            place = jnp.concatenate([jnp.where(here, 1.0, 0.0), none], axis=1)
            weight = jnp.concatenate([none, jnp.where(here, plan_ref[j, 2 * e + 1 : 2 * e + 2, :], 0.0)], axis=1)
            picks = jnp.concatenate([place, weight]).astype(BF16)
            picked.append(dot(picks, blocks[j][...]))
        span = pl.ds(pl.multiple_of(step * sources * capacity, sources * capacity), sources * capacity)
        x[span, :] = jnp.concatenate([pair[:capacity] for pair in picked]).astype(BF16)
        sc[span, :] = jnp.concatenate([pair[capacity:] for pair in picked]).astype(BF16)

    for part in range(2):
        span = slice(part * rows // 2, (part + 1) * rows // 2)

        @pl.when(step == (part + 1) * steps // 2 - 1)
        def _():
            xt[:, span] = x[span, :].T
            if last:
                st[:, span] = sc[span, :].T
                old_st[:, span] = old_scaled_ref[span, :].T

    if not last:

        @pl.when(step == steps)
        def _():
            keep.start()

    @pl.when(step >= steps)
    def _():
        pre_gate = dot(x[...], gate_ref[...])
        pre_up = dot(x[...], up_ref[...])
        grad_hidden = dot(sc[...], down_ref[...], CONTRACT_LAST)
        s = jax.nn.sigmoid(pre_gate)
        activation = pre_gate * s
        hidden = (activation * pre_up).astype(BF16)
        grad_pregate = (grad_hidden * pre_up * (s * (1.0 + pre_gate * (1.0 - s)))).astype(BF16)
        grad_preup = (grad_hidden * activation).astype(BF16)
        hidden_ref[...] = hidden
        pregate_ref[...] = grad_pregate
        preup_ref[...] = grad_preup
        pairs = [(xt, grad_pregate), (xt, grad_preup)]
        if last:
            pairs += [(st, hidden), (old_st, old_hidden_ref[...])]
        for which, (left, right) in enumerate(pairs):
            product = dot(left[...], right).astype(BF16)
            for r in range(shards):
                grads_ref[r, which] = product[r * shard_rows : (r + 1) * shard_rows]

    if not last:

        @pl.when(step == pl.num_programs(0) - 1)
        def _():
            keep.wait()


def expert_grads(gathered, plan, gate_proj, up_proj, down_proj, e, capacity, shards, old):
    group, height, model_dim = gathered.shape
    rows = group * capacity
    hidden_dim = gate_proj.shape[2]
    tile = 256
    sources = 4
    steps = group // sources

    def at(s):
        return jnp.maximum(s - steps, 0)

    def source(j):
        return lambda s: (jnp.minimum(s, steps - 1) * sources + j, 0, 0)

    narrow = pl.BlockSpec((rows, tile), lambda s: (0, at(s)))
    last = old is not None
    matrices = 4 if last else 2
    wide = pltpu.VMEM((rows, model_dim), BF16)
    tall = pltpu.VMEM((model_dim, rows), BF16)
    return pl.pallas_call(
        functools.partial(grads_kernel, steps, sources, e, last),
        grid=(steps + hidden_dim // tile,),
        in_specs=[
            pl.BlockSpec((sources, *plan.shape[1:]), lambda s: (jnp.minimum(s, steps - 1), 0, 0)),
            *[pl.BlockSpec((None, height, model_dim), source(j)) for j in range(sources)],
            pl.BlockSpec((None, model_dim, tile), lambda s: (e, 0, at(s))),
            pl.BlockSpec((None, model_dim, tile), lambda s: (e, 0, at(s))),
            pl.BlockSpec((None, tile, model_dim), lambda s: (e, at(s), 0)),
        ]
        + [narrow, pl.BlockSpec((rows, model_dim), lambda s: (0, 0), pipeline_mode=pl.Buffered(1))] * last,
        out_specs=[
            pl.BlockSpec((shards, matrices, model_dim // shards, tile), lambda s: (0, 0, 0, at(s))),
            narrow,
            narrow,
            narrow,
        ]
        + [pl.BlockSpec(memory_space=pl.ANY)] * (not last),
        out_shape=[jax.ShapeDtypeStruct((shards, matrices, model_dim // shards, hidden_dim), BF16)]
        + [jax.ShapeDtypeStruct((rows, hidden_dim), BF16)] * 3
        + [jax.ShapeDtypeStruct((rows, model_dim), BF16)] * (not last),
        scratch_shapes=[wide, tall, wide] + ([tall, tall] if last else [pltpu.SemaphoreType.DMA]),
        compiler_params=pltpu.CompilerParams(vmem_limit_bytes=61 << 20),
        cost_estimate=pl.CostEstimate(
            flops=12 * rows * model_dim * hidden_dim,
            bytes_accessed=2 * gathered.size + 12 * model_dim * hidden_dim + 6 * rows * hidden_dim,
            transcendentals=rows * hidden_dim,
        ),
    )(plan, *[gathered] * sources, gate_proj, up_proj, down_proj, *(old if last else ()))


def returns_kernel(hidden_ref, pregate_ref, preup_ref, gate_ref, up_ref, down_ref, back_ref):
    group, height, _ = back_ref.shape
    capacity = height // 2
    out = dot(hidden_ref[...], down_ref[...])
    part = dot(pregate_ref[...], gate_ref[...], CONTRACT_LAST) + dot(preup_ref[...], up_ref[...], CONTRACT_LAST)
    for source in range(group):
        rows = slice(source * capacity, (source + 1) * capacity)
        pieces = [v[rows][span] for span in (slice(0, 16), slice(16, capacity)) for v in (out, part)]
        back_ref[source] = jnp.concatenate(pieces).astype(BF16)


def expert_returns(hidden, pregate, preup, gate_proj, up_proj, down_proj, e, group):
    rows, hidden_dim = hidden.shape
    model_dim = gate_proj.shape[1]
    capacity = rows // group
    tile = 512
    whole = pl.BlockSpec((rows, hidden_dim), lambda d: (0, 0), pipeline_mode=pl.Buffered(1))
    return pl.pallas_call(
        returns_kernel,
        grid=(model_dim // tile,),
        in_specs=[
            whole,
            whole,
            whole,
            pl.BlockSpec((None, tile, hidden_dim), lambda d: (e, d, 0)),
            pl.BlockSpec((None, tile, hidden_dim), lambda d: (e, d, 0)),
            pl.BlockSpec((None, hidden_dim, tile), lambda d: (e, 0, d)),
        ],
        out_specs=pl.BlockSpec((group, 2 * capacity, tile), lambda d: (0, 0, d)),
        out_shape=jax.ShapeDtypeStruct((group, 2 * capacity, model_dim), BF16),
        compiler_params=pltpu.CompilerParams(vmem_limit_bytes=60 << 20),
        cost_estimate=pl.CostEstimate(
            flops=600 * rows * model_dim * hidden_dim,
            bytes_accessed=4 * rows * model_dim + 6 * model_dim * hidden_dim + 6 * rows * hidden_dim,
            transcendentals=0,
        ),
    )(hidden, pregate, preup, gate_proj, up_proj, down_proj)


def finish_kernel(experts, cotangent_ref, *refs):
    pairs, reduced = refs[: 2 * experts], refs[2 * experts : 3 * experts]
    combined_ref, tokens_ref, products_ref, gate_ref, up_ref, down_ref, total = refs[3 * experts :]
    tok_dev = combined_ref.shape[0]
    devices, height, model_dim = pairs[0].shape
    step = pl.program_id(0)

    for e in range(experts):
        gate_ref[e] = reduced[e][0]
        up_ref[e] = reduced[e][1]
    down_ref[0] = reduced[1][3].T
    down_ref[1] = reduced[1][2].T

    sums = None
    for e in range(experts):
        rows = pairs[2 * e][...].reshape(devices * height, model_dim)
        picks = pairs[2 * e + 1][...]
        part = dot(picks, rows, CONTRACT_FIRST)
        sums = part if sums is None else sums + part
        gates = picks[:, :tok_dev].reshape(devices, height, tok_dev)
        by_device = []
        for span in (slice(0, 16), slice(32, 48)):
            product = dot(pairs[2 * e][:, span, :].reshape(devices * 16, model_dim), cotangent_ref[...], CONTRACT_LAST)
            given = gates[:, span, :].reshape(devices * 16, tok_dev).astype(F32)
            by_device.append(jnp.where(given > 0.0, product, 0.0))
        for d in range(devices):
            rows_d = slice(d * 16, (d + 1) * 16)
            products_ref[e, d] = jnp.sum(by_device[0][rows_d] + by_device[1][rows_d], axis=0, keepdims=True)

    @pl.when(step == 0)
    def _():
        total[...] = sums

    @pl.when(step > 0)
    def _():
        total[...] += sums

    @pl.when(step == pl.num_programs(0) - 1)
    def _():
        combined_ref[...] = total[:tok_dev].astype(BF16)
        tokens_ref[...] = total[tok_dev:].astype(BF16)


def finish(cotangent, returned, picks, reduced):
    experts = len(returned)
    group, height, model_dim = returned[0].shape
    tok_dev = cotangent.shape[0]
    _, shard_rows, hidden_dim = reduced[0].shape
    steps = 2
    step, tile = group // steps, hidden_dim // steps
    whole = pl.BlockSpec((tok_dev, model_dim), lambda s: (0, 0))
    straight = pl.BlockSpec((experts, shard_rows, tile), lambda s: (0, 0, s))
    return pl.pallas_call(
        functools.partial(finish_kernel, experts),
        grid=(steps,),
        in_specs=[whole]
        + [
            pl.BlockSpec((step, height, model_dim), lambda s: (s, 0, 0)),
            pl.BlockSpec((step * height, 2 * tok_dev), lambda s: (s, 0)),
        ]
        * experts
        + [pl.BlockSpec((v.shape[0], shard_rows, tile), lambda s: (0, 0, s)) for v in reduced],
        out_specs=[
            whole,
            whole,
            pl.BlockSpec((experts, step, 1, tok_dev), lambda s: (0, s, 0, 0)),
            straight,
            straight,
            pl.BlockSpec((experts, tile, shard_rows), lambda s: (0, s, 0)),
        ],
        out_shape=[
            jax.ShapeDtypeStruct((tok_dev, model_dim), BF16),
            jax.ShapeDtypeStruct((tok_dev, model_dim), BF16),
            jax.ShapeDtypeStruct((experts, group, 1, tok_dev), F32),
            jax.ShapeDtypeStruct((experts, shard_rows, hidden_dim), BF16),
            jax.ShapeDtypeStruct((experts, shard_rows, hidden_dim), BF16),
            jax.ShapeDtypeStruct((experts, hidden_dim, shard_rows), BF16),
        ],
        scratch_shapes=[pltpu.VMEM((2 * tok_dev, model_dim), F32)],
        compiler_params=pltpu.CompilerParams(vmem_limit_bytes=60 << 20),
        cost_estimate=pl.CostEstimate(
            flops=6 * experts * group * height * tok_dev * model_dim,
            bytes_accessed=2 * experts * (group * height * (model_dim + 2 * tok_dev) + 6 * shard_rows * hidden_dim),
            transcendentals=0,
        ),
    )(cotangent, *[v for pair in zip(returned, picks) for v in pair], *reduced)


def exchange(rows):
    return lax.all_to_all(rows, "expert", split_axis=0, concat_axis=0, tiled=True)


def local(tokens, cotangent, expert_ids, gate_weights, token_counts, gate_proj, up_proj, down_proj):
    group = lax.axis_size("expert")
    shards = lax.axis_size("dp")
    local_experts, model_dim, hidden_dim = gate_proj.shape
    tok_dev, top = expert_ids.shape
    experts_total = group * local_experts
    capacity = 3 * tok_dev * top // (2 * experts_total)

    live = lax.broadcasted_iota(jnp.int32, (tok_dev, top), 0) < token_counts[0]
    named = jnp.where(live, expert_ids, NOBODY)
    gathered = lax.all_gather(jnp.concatenate([tokens, cotangent])[None], "expert", axis=0, tiled=True)

    labels = lax.broadcasted_iota(jnp.int32, (experts_total, 1, 1), 0)
    hits = named.T[None] == labels
    names = jnp.any(hits, axis=1)
    gates = jnp.sum(jnp.where(hits, gate_weights.T[None].astype(F32), 0.0), axis=1)
    before = (
        lax.broadcasted_iota(jnp.int32, (tok_dev, tok_dev), 0)
        < lax.broadcasted_iota(jnp.int32, (tok_dev, tok_dev), 1)
    )
    rank = dot(names.astype(BF16), before.astype(BF16)).astype(jnp.int32)
    names, gates, rank = (v.reshape(group, local_experts, 1, tok_dev) for v in (names, gates, rank))
    column = lax.broadcasted_iota(jnp.int32, (1, 2 * capacity, 1), 1)
    rest = 32 + capacity - 16
    out_slot = jnp.where(column < 16, column, jnp.where((column >= 32) & (column < rest), column - 16, -1))
    part_slot = jnp.where(column >= rest, column - rest + 16, jnp.where((column >= 16) & (column < 32), column - 16, -1))
    picks = []
    for e in range(local_experts):
        place = names[:, e] & (rank[:, e] == out_slot)
        second = names[:, e] & (rank[:, e] == part_slot)
        picks.append(
            jnp.concatenate([jnp.where(place, gates[:, e], 0.0).astype(BF16), second.astype(BF16)], axis=2)
            .reshape(-1, 2 * tok_dev)
        )

    slots = jnp.where(names, rank.astype(F32), -1.0)
    plan = jnp.concatenate([slots, gates], axis=2).reshape(group, 2 * local_experts, tok_dev)
    plan = exchange(jnp.pad(plan, ((0, 0), (0, 8 - 2 * local_experts), (0, 0))))
    gathered, plan, *picks = lax.optimization_barrier((gathered, plan, *picks))
    old = None

    returned, reduced = [], []
    for e in range(local_experts):
        grads, hidden, pregate, preup, *scaled = expert_grads(
            gathered, plan, gate_proj, up_proj, down_proj, e, capacity, shards, old
        )
        old = (hidden, *scaled)
        reduced.append(lax.psum_scatter(grads, "dp", scatter_dimension=0, tiled=False))
        back = expert_returns(hidden, pregate, preup, gate_proj, up_proj, down_proj, e, group)
        returned.append(exchange(back))

    combined, tokens_grad, products, *weight_grads = finish(cotangent, returned, picks, reduced)
    per_expert = products.transpose(1, 0, 2, 3).reshape(experts_total, 1, tok_dev)
    gates_grad = jnp.sum(jnp.where(hits, per_expert, 0.0), axis=0).T
    return (
        combined,
        tokens_grad,
        gates_grad.astype(BF16),
        *weight_grads,
    )


def solution(mesh):
    both = ("dp", "expert")
    return jax.shard_map(
        local,
        mesh=mesh,
        in_specs=(
            P(both, None),
            P(both, None),
            P(both, None),
            P(both, None),
            P(both),
            P("expert", None, None),
            P("expert", None, None),
            P("expert", None, None),
        ),
        out_specs=(
            P(both, None),
            P(both, None),
            P(both, None),
            P("expert", "dp", None),
            P("expert", "dp", None),
            P("expert", None, "dp"),
        ),
        check_vma=False,
    )
```

```python
import functools

import jax
import jax.numpy as jnp
from jax import lax
from jax.experimental import pallas as pl
from jax.experimental.pallas import tpu as pltpu
from jax.sharding import PartitionSpec as P

F32 = jnp.float32
BF16 = jnp.bfloat16
CONTRACT_FIRST = (((0,), (0,)), ((), ()))
CONTRACT_LAST = (((1,), (1,)), ((), ()))
NOBODY = -1


def dot(a, b, dims=(((1,), (0,)), ((), ()))):
    return lax.dot_general(a, b, dims, preferred_element_type=F32)


def grads_kernel(steps, sources, e, last, plan_ref, *refs):
    blocks, (gate_ref, up_ref, down_ref), refs = refs[:sources], refs[sources : sources + 3], refs[sources + 3 :]
    if last:
        old_hidden_ref, old_scaled_ref, grads_ref, hidden_ref, pregate_ref, preup_ref, x, xt, sc, st, old_st = refs
    else:
        grads_ref, hidden_ref, pregate_ref, preup_ref, scaled_ref, x, xt, sc, sem = refs
        keep = pltpu.make_async_copy(sc, scaled_ref, sem)
    step = pl.program_id(0)
    tok_dev = plan_ref.shape[2]
    rows, model_dim = x.shape
    capacity = rows // (steps * sources)
    shards, _, shard_rows, _ = grads_ref.shape

    @pl.when(step < steps)
    def _():
        column = lax.broadcasted_iota(jnp.int32, (capacity, tok_dev), 0).astype(F32)
        none = jnp.zeros((capacity, tok_dev), F32)
        picked = []
        for j in range(sources):
            here = plan_ref[j, 2 * e : 2 * e + 1, :] == column
            place = jnp.concatenate([jnp.where(here, 1.0, 0.0), none], axis=1)
            weight = jnp.concatenate([none, jnp.where(here, plan_ref[j, 2 * e + 1 : 2 * e + 2, :], 0.0)], axis=1)
            picks = jnp.concatenate([place, weight]).astype(BF16)
            picked.append(dot(picks, blocks[j][...]))
        span = pl.ds(pl.multiple_of(step * sources * capacity, sources * capacity), sources * capacity)
        x[span, :] = jnp.concatenate([pair[:capacity] for pair in picked]).astype(BF16)
        sc[span, :] = jnp.concatenate([pair[capacity:] for pair in picked]).astype(BF16)

    for part in range(2):
        span = slice(part * rows // 2, (part + 1) * rows // 2)

        @pl.when(step == (part + 1) * steps // 2 - 1)
        def _():
            xt[:, span] = x[span, :].T
            if last:
                st[:, span] = sc[span, :].T
                old_st[:, span] = old_scaled_ref[span, :].T

    if not last:

        @pl.when(step == steps)
        def _():
            keep.start()

    @pl.when(step >= steps)
    def _():
        pre_gate = dot(x[...], gate_ref[...])
        pre_up = dot(x[...], up_ref[...])
        grad_hidden = dot(sc[...], down_ref[...], CONTRACT_LAST)
        s = jax.nn.sigmoid(pre_gate)
        activation = pre_gate * s
        hidden = (activation * pre_up).astype(BF16)
        grad_pregate = (grad_hidden * pre_up * (s * (1.0 + pre_gate * (1.0 - s)))).astype(BF16)
        grad_preup = (grad_hidden * activation).astype(BF16)
        hidden_ref[...] = hidden
        pregate_ref[...] = grad_pregate
        preup_ref[...] = grad_preup
        pairs = [(xt, grad_pregate), (xt, grad_preup)]
        if last:
            pairs += [(st, hidden), (old_st, old_hidden_ref[...])]
        for which, (left, right) in enumerate(pairs):
            product = dot(left[...], right).astype(BF16)
            for r in range(shards):
                grads_ref[r, which] = product[r * shard_rows : (r + 1) * shard_rows]

    if not last:

        @pl.when(step == pl.num_programs(0) - 1)
        def _():
            keep.wait()


def expert_grads(gathered, plan, gate_proj, up_proj, down_proj, e, capacity, shards, old):
    group, height, model_dim = gathered.shape
    rows = group * capacity
    hidden_dim = gate_proj.shape[2]
    tile = 256
    sources = 4
    steps = group // sources

    def at(s):
        return jnp.maximum(s - steps, 0)

    def source(j):
        return lambda s: (jnp.minimum(s, steps - 1) * sources + j, 0, 0)

    narrow = pl.BlockSpec((rows, tile), lambda s: (0, at(s)))
    last = old is not None
    matrices = 4 if last else 2
    wide = pltpu.VMEM((rows, model_dim), BF16)
    tall = pltpu.VMEM((model_dim, rows), BF16)
    return pl.pallas_call(
        functools.partial(grads_kernel, steps, sources, e, last),
        grid=(steps + hidden_dim // tile,),
        in_specs=[
            pl.BlockSpec((sources, *plan.shape[1:]), lambda s: (jnp.minimum(s, steps - 1), 0, 0)),
            *[pl.BlockSpec((None, height, model_dim), source(j)) for j in range(sources)],
            pl.BlockSpec((None, model_dim, tile), lambda s: (e, 0, at(s))),
            pl.BlockSpec((None, model_dim, tile), lambda s: (e, 0, at(s))),
            pl.BlockSpec((None, tile, model_dim), lambda s: (e, at(s), 0)),
        ]
        + [narrow, pl.BlockSpec((rows, model_dim), lambda s: (0, 0), pipeline_mode=pl.Buffered(1))] * last,
        out_specs=[
            pl.BlockSpec((shards, matrices, model_dim // shards, tile), lambda s: (0, 0, 0, at(s))),
            narrow,
            narrow,
            narrow,
        ]
        + [pl.BlockSpec(memory_space=pl.ANY)] * (not last),
        out_shape=[jax.ShapeDtypeStruct((shards, matrices, model_dim // shards, hidden_dim), BF16)]
        + [jax.ShapeDtypeStruct((rows, hidden_dim), BF16)] * 3
        + [jax.ShapeDtypeStruct((rows, model_dim), BF16)] * (not last),
        scratch_shapes=[wide, tall, wide] + ([tall, tall] if last else [pltpu.SemaphoreType.DMA]),
        compiler_params=pltpu.CompilerParams(vmem_limit_bytes=61 << 20),
        cost_estimate=pl.CostEstimate(
            flops=12 * rows * model_dim * hidden_dim,
            bytes_accessed=2 * gathered.size + 12 * model_dim * hidden_dim + 6 * rows * hidden_dim,
            transcendentals=rows * hidden_dim,
        ),
    )(plan, *[gathered] * sources, gate_proj, up_proj, down_proj, *(old if last else ()))


def returns_kernel(hidden_ref, pregate_ref, preup_ref, gate_ref, up_ref, down_ref, back_ref):
    group, height, _ = back_ref.shape
    capacity = height // 2
    out = dot(hidden_ref[...], down_ref[...])
    part = dot(pregate_ref[...], gate_ref[...], CONTRACT_LAST) + dot(preup_ref[...], up_ref[...], CONTRACT_LAST)
    for source in range(group):
        rows = slice(source * capacity, (source + 1) * capacity)
        pieces = [v[rows][span] for span in (slice(0, 16), slice(16, capacity)) for v in (out, part)]
        back_ref[source] = jnp.concatenate(pieces).astype(BF16)


def expert_returns(hidden, pregate, preup, gate_proj, up_proj, down_proj, e, group):
    rows, hidden_dim = hidden.shape
    model_dim = gate_proj.shape[1]
    capacity = rows // group
    tile = 256
    whole = pl.BlockSpec((rows, hidden_dim), lambda d: (0, 0), pipeline_mode=pl.Buffered(1))
    return pl.pallas_call(
        returns_kernel,
        grid=(model_dim // tile,),
        in_specs=[
            whole,
            whole,
            whole,
            pl.BlockSpec((None, tile, hidden_dim), lambda d: (e, d, 0)),
            pl.BlockSpec((None, tile, hidden_dim), lambda d: (e, d, 0)),
            pl.BlockSpec((None, hidden_dim, tile), lambda d: (e, 0, d)),
        ],
        out_specs=pl.BlockSpec((group, 2 * capacity, tile), lambda d: (0, 0, d)),
        out_shape=jax.ShapeDtypeStruct((group, 2 * capacity, model_dim), BF16),
        compiler_params=pltpu.CompilerParams(vmem_limit_bytes=60 << 20),
        cost_estimate=pl.CostEstimate(
            flops=600 * rows * model_dim * hidden_dim,
            bytes_accessed=4 * rows * model_dim + 6 * model_dim * hidden_dim + 6 * rows * hidden_dim,
            transcendentals=0,
        ),
    )(hidden, pregate, preup, gate_proj, up_proj, down_proj)


def finish_kernel(experts, cotangent_ref, *refs):
    pairs, reduced = refs[: 2 * experts], refs[2 * experts : 3 * experts]
    combined_ref, tokens_ref, products_ref, gate_ref, up_ref, down_ref, total = refs[3 * experts :]
    tok_dev = combined_ref.shape[0]
    devices, height, model_dim = pairs[0].shape
    step = pl.program_id(0)

    for e in range(experts):
        gate_ref[e] = reduced[e][0]
        up_ref[e] = reduced[e][1]
    down_ref[0] = reduced[1][3].T
    down_ref[1] = reduced[1][2].T

    sums = None
    for e in range(experts):
        rows = pairs[2 * e][...].reshape(devices * height, model_dim)
        picks = pairs[2 * e + 1][...]
        part = dot(picks, rows, CONTRACT_FIRST)
        sums = part if sums is None else sums + part
        gates = picks[:, :tok_dev].reshape(devices, height, tok_dev)
        by_device = []
        for span in (slice(0, 16), slice(32, 48)):
            product = dot(pairs[2 * e][:, span, :].reshape(devices * 16, model_dim), cotangent_ref[...], CONTRACT_LAST)
            given = gates[:, span, :].reshape(devices * 16, tok_dev).astype(F32)
            by_device.append(jnp.where(given > 0.0, product, 0.0))
        for d in range(devices):
            rows_d = slice(d * 16, (d + 1) * 16)
            products_ref[e, d] = jnp.sum(by_device[0][rows_d] + by_device[1][rows_d], axis=0, keepdims=True)

    @pl.when(step == 0)
    def _():
        total[...] = sums

    @pl.when(step > 0)
    def _():
        total[...] += sums

    @pl.when(step == pl.num_programs(0) - 1)
    def _():
        combined_ref[...] = total[:tok_dev].astype(BF16)
        tokens_ref[...] = total[tok_dev:].astype(BF16)


def finish(cotangent, returned, picks, reduced):
    experts = len(returned)
    group, height, model_dim = returned[0].shape
    tok_dev = cotangent.shape[0]
    _, shard_rows, hidden_dim = reduced[0].shape
    steps = 2
    step, tile = group // steps, hidden_dim // steps
    whole = pl.BlockSpec((tok_dev, model_dim), lambda s: (0, 0))
    straight = pl.BlockSpec((experts, shard_rows, tile), lambda s: (0, 0, s))
    return pl.pallas_call(
        functools.partial(finish_kernel, experts),
        grid=(steps,),
        in_specs=[whole]
        + [
            pl.BlockSpec((step, height, model_dim), lambda s: (s, 0, 0)),
            pl.BlockSpec((step * height, 2 * tok_dev), lambda s: (s, 0)),
        ]
        * experts
        + [pl.BlockSpec((v.shape[0], shard_rows, tile), lambda s: (0, 0, s)) for v in reduced],
        out_specs=[
            whole,
            whole,
            pl.BlockSpec((experts, step, 1, tok_dev), lambda s: (0, s, 0, 0)),
            straight,
            straight,
            pl.BlockSpec((experts, tile, shard_rows), lambda s: (0, s, 0)),
        ],
        out_shape=[
            jax.ShapeDtypeStruct((tok_dev, model_dim), BF16),
            jax.ShapeDtypeStruct((tok_dev, model_dim), BF16),
            jax.ShapeDtypeStruct((experts, group, 1, tok_dev), F32),
            jax.ShapeDtypeStruct((experts, shard_rows, hidden_dim), BF16),
            jax.ShapeDtypeStruct((experts, shard_rows, hidden_dim), BF16),
            jax.ShapeDtypeStruct((experts, hidden_dim, shard_rows), BF16),
        ],
        scratch_shapes=[pltpu.VMEM((2 * tok_dev, model_dim), F32)],
        compiler_params=pltpu.CompilerParams(vmem_limit_bytes=60 << 20),
        cost_estimate=pl.CostEstimate(
            flops=6 * experts * group * height * tok_dev * model_dim,
            bytes_accessed=2 * experts * (group * height * (model_dim + 2 * tok_dev) + 6 * shard_rows * hidden_dim),
            transcendentals=0,
        ),
    )(cotangent, *[v for pair in zip(returned, picks) for v in pair], *reduced)


def exchange(rows):
    return lax.all_to_all(rows, "expert", split_axis=0, concat_axis=0, tiled=True)


def local(tokens, cotangent, expert_ids, gate_weights, token_counts, gate_proj, up_proj, down_proj):
    group = lax.axis_size("expert")
    shards = lax.axis_size("dp")
    local_experts, model_dim, hidden_dim = gate_proj.shape
    tok_dev, top = expert_ids.shape
    experts_total = group * local_experts
    capacity = 3 * tok_dev * top // (2 * experts_total)

    live = lax.broadcasted_iota(jnp.int32, (tok_dev, top), 0) < token_counts[0]
    named = jnp.where(live, expert_ids, NOBODY)
    gathered = lax.all_gather(jnp.concatenate([tokens, cotangent])[None], "expert", axis=0, tiled=True)

    labels = lax.broadcasted_iota(jnp.int32, (experts_total, 1, 1), 0)
    hits = named.T[None] == labels
    names = jnp.any(hits, axis=1)
    gates = jnp.sum(jnp.where(hits, gate_weights.T[None].astype(F32), 0.0), axis=1)
    before = (
        lax.broadcasted_iota(jnp.int32, (tok_dev, tok_dev), 0)
        < lax.broadcasted_iota(jnp.int32, (tok_dev, tok_dev), 1)
    )
    rank = dot(names.astype(BF16), before.astype(BF16)).astype(jnp.int32)
    names, gates, rank = (v.reshape(group, local_experts, 1, tok_dev) for v in (names, gates, rank))
    column = lax.broadcasted_iota(jnp.int32, (1, 2 * capacity, 1), 1)
    rest = 32 + capacity - 16
    out_slot = jnp.where(column < 16, column, jnp.where((column >= 32) & (column < rest), column - 16, -1))
    part_slot = jnp.where(column >= rest, column - rest + 16, jnp.where((column >= 16) & (column < 32), column - 16, -1))
    picks = []
    for e in range(local_experts):
        place = names[:, e] & (rank[:, e] == out_slot)
        second = names[:, e] & (rank[:, e] == part_slot)
        picks.append(
            jnp.concatenate([jnp.where(place, gates[:, e], 0.0).astype(BF16), second.astype(BF16)], axis=2)
            .reshape(-1, 2 * tok_dev)
        )

    slots = jnp.where(names, rank.astype(F32), -1.0)
    plan = jnp.concatenate([slots, gates], axis=2).reshape(group, 2 * local_experts, tok_dev)
    plan = exchange(jnp.pad(plan, ((0, 0), (0, 8 - 2 * local_experts), (0, 0))))
    gathered, plan, *picks = lax.optimization_barrier((gathered, plan, *picks))
    old = None

    returned, reduced = [], []
    for e in range(local_experts):
        grads, hidden, pregate, preup, *scaled = expert_grads(
            gathered, plan, gate_proj, up_proj, down_proj, e, capacity, shards, old
        )
        old = (hidden, *scaled)
        reduced.append(lax.psum_scatter(grads, "dp", scatter_dimension=0, tiled=False))
        back = expert_returns(hidden, pregate, preup, gate_proj, up_proj, down_proj, e, group)
        returned.append(exchange(back))

    combined, tokens_grad, products, *weight_grads = finish(cotangent, returned, picks, reduced)
    per_expert = products.transpose(1, 0, 2, 3).reshape(experts_total, 1, tok_dev)
    gates_grad = jnp.sum(jnp.where(hits, per_expert, 0.0), axis=0).T
    return (
        combined,
        tokens_grad,
        gates_grad.astype(BF16),
        *weight_grads,
    )


def solution(mesh):
    both = ("dp", "expert")
    return jax.shard_map(
        local,
        mesh=mesh,
        in_specs=(
            P(both, None),
            P(both, None),
            P(both, None),
            P(both, None),
            P(both),
            P("expert", None, None),
            P("expert", None, None),
            P("expert", None, None),
        ),
        out_specs=(
            P(both, None),
            P(both, None),
            P(both, None),
            P("expert", "dp", None),
            P("expert", "dp", None),
            P("expert", None, "dp"),
        ),
        check_vma=False,
    )
```
